128 devices in a mesh: section: 2 (over y_lo), expert: 16 (over x, z), shard: 4 (over y_hi, core).
Axes of the slice: x: 4, y: 4 (y_hi: 2, y_lo: 2; y = y_hi * 2 + y_lo), z: 4, core: 2. Of those that a mesh axis runs over, the one named last changes fastest.
Arguments:
- stream: bfloat16 [2, 2, 8192, 768], P('section', None, ('expert', 'shard')), may hold values from -6 to 6
- norm_gains: float32 [2, 2, 768], P('section'), may hold values from 0.25 to 1.75
- attn_qkv: bfloat16 [2, 3, 768, 768], P('section', None, None, 'shard'), may hold values from -0.21875 to 0.21875
- attn_out: bfloat16 [2, 768, 768], P('section', 'shard'), may hold values from -3.5 to 3.5
- rel_bias: float32 [2, 32, 12], P('section', None, 'shard'), may hold values from -4 to 4
- router: bfloat16 [2, 768, 32], P('section'), may hold values from -0.21875 to 0.21875
- expert_in: bfloat16 [2, 32, 768, 3072], P('section', 'expert', None, 'shard'), may hold values from -0.21875 to 0.21875
- expert_out: bfloat16 [2, 32, 3072, 768], P('section', 'expert', 'shard'), may hold values from -3.5 to 3.5
- routes: int32 [2, 2, 8192], P('section', None, ('expert', 'shard')), may hold values from 0 to 31, as said below
- slots: int32 [2, 2, 8192], P('section', None, ('expert', 'shard')), may hold values from 0 to 5, as said below
Outputs:
- end_rows: bfloat16 [2, 2, 8192, 768], P('section', None, ('expert', 'shard'))
- grad_gains: float32 [2, 2, 768], P('section')
- grad_qkv: float32 [2, 3, 768, 768], P('section', None, None, 'shard')
- grad_attn_out: float32 [2, 768, 768], P('section', 'shard')
- grad_bias: float32 [2, 32, 12], P('section', None, 'shard')
- grad_router: float32 [2, 768, 32], P('section')
- grad_expert_in: float32 [2, 32, 768, 3072], P('section', 'expert', None, 'shard')
- grad_expert_out: float32 [2, 32, 3072, 768], P('section', 'expert', 'shard')
The draws below stay inside these ranges and needn't reach their ends.
Inputs may be any that keep to these rules, and one draw needn't show every extreme that they name: `routes`: within the rows of one device in one micro-batch (aligned blocks of 128 rows), each expert is named at most 6 times; in every micro-batch of every layer one expert is named exactly 6 times by the rows of every device. Rows of one device in one micro-batch that name the same expert hold distinct slots.
All inputs are finite; a program needn't handle non-finite values.
Results may differ from the reference program's by a relative error of at most 0.04.
Values may be sent and summed in bfloat16 or wider, within the bound.
A program may use at most 192 MiB of HBM per device.

```python
import jax
import jax.numpy as jnp
from jax import lax

D = 768
HEADS = 12
HEAD_DIM = 64
FF = 3072
BUCKETS = 32
LEN = 512
MB = 2
EXPERTS = 32
TOKG = 8192
ROWS = 128
CAPD = 6


def route_table(key):
    per_layer = TOKG // ROWS
    block_total = 2 * MB * per_layer
    slot_total = EXPERTS * CAPD
    key_jitter, key_lean, key_busy, key_order = jax.random.split(key, 4)
    jitter = jax.random.randint(key_jitter, (block_total, EXPERTS, CAPD), 0, 65536)
    expert_lean = jax.random.randint(key_lean, (block_total, EXPERTS, 1), 0, 65536)
    busiest = jnp.repeat(jax.random.randint(key_busy, (2 * MB, 1, 1), 0, EXPERTS), per_layer, axis=0)
    expert_ids = jnp.arange(EXPERTS, dtype=jnp.int32)[None, :, None]
    scores = jnp.where(expert_ids == busiest, -1, jitter + expert_lean)
    ranking = scores.reshape(block_total, slot_total) * slot_total + jnp.arange(slot_total, dtype=jnp.int32)[None, :]
    chosen = jnp.argsort(ranking, axis=1)[:, :ROWS]
    token_order = jax.random.randint(key_order, (block_total, ROWS), 0, 65536) * ROWS + jnp.arange(ROWS, dtype=jnp.int32)[None, :]
    placed = jnp.take_along_axis(chosen, jnp.argsort(token_order, axis=1), axis=1)
    expert_of = (placed // CAPD).reshape(2, MB, TOKG).astype(jnp.int32)
    slot_of = (placed % CAPD).reshape(2, MB, TOKG).astype(jnp.int32)
    return (expert_of, slot_of)


def draw_routes(key, part):
    return route_table(key)[0]


def draw_slots(key, part):
    return route_table(key)[1]


def level_of(stream_key, shape, cuts, low, largest):
    level = 1.0
    for axis_at, parts in cuts:
        draws = jax.random.uniform(jax.random.fold_in(jax.random.fold_in(stream_key, 6), axis_at), (parts,), jnp.float32, low / len(cuts), largest / len(cuts))
        level = level * jnp.repeat(jnp.exp(draws), shape[axis_at] // parts).reshape((-1,) + (1,) * (len(shape) - 1 - axis_at))
    return level


def scatter_about(key, extent, spread, most, pieces=(), held_as=jnp.bfloat16):
    values = jax.random.normal(key, extent, jnp.float32) * spread
    if len(pieces) > 0:
        values = level_of(key, extent, pieces, -0.22, 0.18) * values
    return jnp.clip(values, min=-most, max=most).astype(held_as)


def setup_inputs(seed: int = 0) -> dict:
    key_list = jax.random.split(jax.random.key(seed), 11)
    return {
        "stream": scatter_about(key_list[0], (2, MB, TOKG, D), 1.0, 6.0, ((0, 2), (2, 64))),
        "norm_gains": jnp.clip(1.0 + 0.15 * jax.random.normal(key_list[1], (2, 2, D), jnp.float32), 0.25, 1.75),
        "attn_qkv": scatter_about(key_list[2], (2, 3, D, HEADS * HEAD_DIM), D ** -0.5, 0.21875, ((0, 2), (3, 4))),
        "attn_out": scatter_about(key_list[3], (2, HEADS * HEAD_DIM, D), (max(2 * HEADS * HEAD_DIM // LEN, 1)) ** -0.5, 3.5, ((0, 2), (1, 4))),
        "rel_bias": scatter_about(key_list[4], (2, BUCKETS, HEADS), 1.0, 4.0, ((0, 2), (2, 4)), jnp.float32),
        "router": scatter_about(key_list[5], (2, D, EXPERTS), D ** -0.5, 0.21875, ((0, 2),)),
        "expert_in": scatter_about(key_list[6], (2, EXPERTS, D, FF), D ** -0.5, 0.21875, ((0, 2), (1, 16), (3, 4))),
        "expert_out": scatter_about(key_list[7], (2, EXPERTS, FF, D), (max(FF // (EXPERTS * EXPERTS), 1)) ** -0.5, 3.5, ((0, 2), (1, 16), (2, 4))),
        "routes": draw_routes(jax.random.fold_in(key_list[10], 71), 0),
        "slots": draw_slots(jax.random.fold_in(key_list[10], 71), 0),
    }


@jax.custom_vjp
def low(v):
    return lax.optimization_barrier(v.astype(jnp.bfloat16)).astype(jnp.float32)

@jax.custom_vjp
def low_back(v):
    return v

def low_keep(v):
    return (low(v), None)

def low_pass(kept, grad):
    return (grad,)

def back_keep(v):
    return (v, None)

def back_low(kept, grad):
    return (low(grad),)
low.defvjp(low_keep, low_pass)
low_back.defvjp(back_keep, back_low)

def rms_norm(values, gain):
    return values * lax.rsqrt(lax.optimization_barrier(jnp.mean(values * values, axis=-1, keepdims=True)) + 1e-06) * gain

def product(left_side, right_side):
    return jnp.dot(left_side, right_side, precision=lax.Precision.HIGHEST)

def bucket_of(offsets):
    distance = jnp.abs(offsets)
    far_bucket = 8 + sum(((distance >= threshold).astype(jnp.int32) for threshold in (12, 16, 23, 32, 46, 64, 91)))
    near_far = jnp.where(distance < 8, distance, far_bucket)
    return near_far + 16 * (offsets > 0).astype(jnp.int32)

def bias_block(bias_table, first_row, row_count, length):
    span_width = length + row_count - 1
    offsets = jnp.arange(span_width, dtype=jnp.int32) - (row_count - 1) - first_row
    picked_bucket = (bucket_of(offsets)[:, None] == jnp.arange(bias_table.shape[0], dtype=jnp.int32)[None, :]).astype(jnp.float32)
    by_offset = jnp.dot(picked_bucket, bias_table, precision=lax.Precision.HIGHEST).T
    head_count = bias_table.shape[1]
    repeated = jnp.broadcast_to(by_offset[:, None, :], (head_count, row_count, span_width)).reshape(head_count, row_count * span_width)
    skewed = repeated[:, row_count - 1:row_count - 1 + row_count * (span_width - 1)].reshape(head_count, row_count, span_width - 1)
    return skewed[:, :, :length]

def layer(rows_in, layer_weights, route_ids, slot_ids):
    gains, qkv_weight, out_weight, bias_table, router_weight, inner_weight, outer_weight = layer_weights
    total_rows = rows_in.shape[0]
    normed = low(rms_norm(rows_in, gains[0]))
    queries = low_back(low(product(normed, qkv_weight[0]))).reshape(total_rows, HEADS, HEAD_DIM)
    key_rows = low_back(low(product(normed, qkv_weight[1]))).reshape(total_rows, HEADS, HEAD_DIM)
    value_rows = low_back(low(product(normed, qkv_weight[2]))).reshape(total_rows, HEADS, HEAD_DIM)
    block_rows = min(512, LEN)
    per_seq = LEN // block_rows

    def one_block(number):
        seq_start = (number // per_seq * LEN).astype(jnp.int32)
        first_row = (number % per_seq * block_rows).astype(jnp.int32)
        query_block = lax.dynamic_slice_in_dim(queries, seq_start + first_row, block_rows, 0)
        key_block = lax.dynamic_slice_in_dim(key_rows, seq_start, LEN, 0)
        value_block = lax.dynamic_slice_in_dim(value_rows, seq_start, LEN, 0)
        scores = jnp.einsum('qhd,khd->hqk', query_block, key_block, precision=lax.Precision.HIGHEST) * 0.125
        scores = scores + bias_block(bias_table, first_row, block_rows, LEN)
        chances = low(jax.nn.softmax(low_back(scores), axis=-1))
        return jnp.einsum('hqk,khd->qhd', chances, value_block, precision=lax.Precision.HIGHEST)
    mixed_heads = lax.map(jax.checkpoint(one_block), jnp.arange(total_rows // block_rows, dtype=jnp.int32))
    mixed_heads = low_back(low(mixed_heads.reshape(total_rows, HEADS * HEAD_DIM)))
    middle = rows_in + low_back(product(mixed_heads, out_weight))
    normed_two = low(rms_norm(middle, gains[1]))
    router_prob = jax.nn.softmax(low_back(product(normed_two, router_weight)), axis=-1)
    chosen = (route_ids[:, None] == jnp.arange(EXPERTS, dtype=jnp.int32)[None, :]).astype(jnp.float32)
    gating = lax.optimization_barrier(jnp.sum(router_prob * chosen, axis=-1))
    block_ids = jnp.arange(total_rows, dtype=jnp.int32) // ROWS
    block_count = total_rows // ROWS
    buffer = jnp.zeros((block_count, EXPERTS, CAPD, D), jnp.float32).at[block_ids, route_ids, slot_ids].set(low_back(normed_two))
    by_expert = jnp.transpose(buffer, (1, 0, 2, 3)).reshape(EXPERTS, block_count * CAPD, D)

    def one_expert(operands):
        row_set, inner_one, outer_one = operands
        pre_act = low_back(product(row_set, inner_one))
        return product(low(jax.nn.gelu(pre_act, approximate=True)), outer_one)
    results = low_back(low(lax.map(jax.checkpoint(one_expert), (by_expert, inner_weight, outer_weight))))
    returned = jnp.transpose(results.reshape(EXPERTS, block_count, CAPD, D), (1, 0, 2, 3))
    expert_rows = returned[block_ids, route_ids, slot_ids]
    return middle + gating[:, None] * expert_rows

def reference(stream, norm_gains, attn_qkv, attn_out, rel_bias, router, expert_in, expert_out, routes, slots):
    weights = tuple((weight_array.astype(jnp.float32) for weight_array in (norm_gains, attn_qkv, attn_out, rel_bias, router, expert_in, expert_out)))
    totals = None
    input_grads = []
    outputs = []
    for micro in range(MB):
        start_rows = stream[0, micro].astype(jnp.float32)
        cotangent = stream[1, micro].astype(jnp.float32)

        def chain(first_input, section_weights, micro=micro):
            layer_zero = tuple((layer_weight[0] for layer_weight in section_weights))
            layer_one = tuple((layer_weight[1] for layer_weight in section_weights))
            middle_rows = layer(first_input, layer_zero, routes[0, micro], slots[0, micro])
            middle_rows = low_back(low(middle_rows))
            return layer(middle_rows, layer_one, routes[1, micro], slots[1, micro])
        result, pull_back = jax.vjp(chain, start_rows, weights)
        input_grad, weight_grads = pull_back(cotangent)
        totals = weight_grads if totals is None else tuple((first + second for first, second in zip(totals, weight_grads)))
        input_grads.append(input_grad)
        outputs.append(result)
    end_rows = jnp.stack([jnp.stack(input_grads), jnp.stack(outputs)]).astype(jnp.bfloat16)
    return (end_rows, totals[0], totals[1], totals[2], totals[3], totals[4], totals[5], totals[6])
```

```python
import functools

import jax
import jax.numpy as jnp
import numpy as np
from jax import lax
from jax.experimental import pallas as pl
from jax.experimental.pallas import tpu as pltpu
from jax.sharding import PartitionSpec as P

HEAD_DIM = 64
HEADS_HERE = 3
LEN = 512
MICRO = 2
ROWS = 128
D = 768
HALF = 384
EXPERTS = 32
CAP = 6
OWNERS = 16
PIECE = 48
VMEM_BYTES = 48 * 1024 * 1024
MESH = pl.DeviceIdType.MESH
ANY = pl.BlockSpec(memory_space=pl.ANY)
VMEM = pl.BlockSpec(memory_space=pltpu.VMEM)


def remote(src, dst, send, recv, axis, index):
    return pltpu.make_async_remote_copy(
        src_ref=src, dst_ref=dst, send_sem=send, recv_sem=recv, device_id={axis: index}, device_id_type=MESH
    )


def greet(partners):
    barrier = pltpu.get_barrier_semaphore()
    for axis, index in partners:
        pl.semaphore_signal(barrier, inc=1, device_id={axis: index}, device_id_type=MESH)
    pl.semaphore_wait(barrier, len(partners))


def shard_places():
    me = lax.axis_index("shard")
    y, core = lax.div(me, 2), lax.rem(me, 2)
    return me, 2 * y + (1 - core), 2 * (1 - y) + core, 2 * (1 - y) + (1 - core)


def expert_places():
    me = lax.axis_index("expert")
    return me, lax.div(me, 4), lax.rem(me, 4)


def owner_at(x, z, dx, dz):
    return lax.rem(x + dx, 4) * 4 + lax.rem(z + dz, 4)


def all_owners(x, z):
    return [("expert", owner_at(x, z, dx, dz)) for dx in range(4) for dz in range(4) if dx or dz]


def when_active(active, old, out, sem, run):
    mine = lax.axis_index("section") == active

    @pl.when(mine)
    def _():
        run()

    if old is not None:

        @pl.when(jnp.logical_not(mine))
        def _():
            keep = pltpu.make_async_copy(old, out, sem)
            keep.start()
            keep.wait()


def gather_kernel(active, kept, x, *refs):
    old = refs[0] if kept else None
    out, local, send, recv = refs[-4:]

    def run():
        me, core, cross, diag = shard_places()
        greet([("shard", core), ("shard", cross)])
        far, near, own, on = [], [], [], []
        for m in range(MICRO):
            far.append(remote(x.at[m], out.at[m, me], send.at[m], recv.at[m], "shard", cross))
            far[m].start()
        for m in range(MICRO):
            near.append(remote(x.at[m], out.at[m, me], send.at[2 + m], recv.at[2 + m], "shard", core))
            near[m].start()
            own.append(pltpu.make_async_copy(x.at[m], out.at[m, me], local.at[m]))
            own[m].start()
        for m in range(MICRO):
            far[m].wait_recv()
            on.append(remote(out.at[m, cross], out.at[m, cross], send.at[4 + m], recv.at[4 + m], "shard", core))
            on[m].start()
        for m in range(MICRO):
            own[m].wait()
            far[m].wait_send()
            near[m].wait()
            on[m].wait()

    when_active(active, old, out, local.at[0], run)


def gather_rows(x, old, active, collective_id):
    return pl.pallas_call(
        functools.partial(gather_kernel, active, old is not None),
        out_shape=jax.ShapeDtypeStruct((MICRO, 4, ROWS, D), jnp.bfloat16),
        in_specs=[ANY] * (1 if old is None else 2),
        out_specs=ANY,
        scratch_shapes=[
            pltpu.SemaphoreType.DMA((2,)),
            pltpu.SemaphoreType.DMA((6,)),
            pltpu.SemaphoreType.DMA((6,)),
        ],
        compiler_params=pltpu.CompilerParams(
            collective_id=collective_id, has_side_effects=True, vmem_limit_bytes=VMEM_BYTES
        ),
        name="gather_rows",
    )(*([x] if old is None else [x, old]))


def scatter_kernel(active, kept, part, *refs):
    old = refs[0] if kept else None
    out, pair, mine, theirs, crossed, local, send, recv = refs[-8:]

    def run():
        me, core, cross, diag = shard_places()
        greet([("shard", core), ("shard", cross)])
        first, second, third = [], [], []
        for m in range(MICRO):
            first.append(remote(part.at[m, diag], theirs.at[m], send.at[m], recv.at[m], "shard", core))
            first[m].start()
        for m in range(MICRO):
            second.append(remote(part.at[m, core], mine.at[m], send.at[2 + m], recv.at[2 + m], "shard", core))
            second[m].start()
        for m in range(MICRO):
            first[m].wait_recv()
            pair[m] = (part[m, cross].astype(jnp.float32) + theirs[m].astype(jnp.float32)).astype(jnp.bfloat16)
            third.append(remote(pair.at[m], crossed.at[m], send.at[4 + m], recv.at[4 + m], "shard", cross))
            third[m].start()
        for m in range(MICRO):
            second[m].wait_recv()
            third[m].wait_recv()
            out[m] = (
                part[m, me].astype(jnp.float32) + mine[m].astype(jnp.float32) + crossed[m].astype(jnp.float32)
            )
        for m in range(MICRO):
            first[m].wait_send()
            second[m].wait_send()
            third[m].wait_send()

    when_active(active, old, out, local, run)


def scatter_rows(part, old, active, collective_id):
    return pl.pallas_call(
        functools.partial(scatter_kernel, active, old is not None),
        out_shape=jax.ShapeDtypeStruct((MICRO, ROWS, D), jnp.float32),
        in_specs=[VMEM] + ([] if old is None else [ANY]),
        out_specs=VMEM,
        scratch_shapes=[pltpu.VMEM((MICRO, ROWS, D), jnp.bfloat16)] * 4
        + [
            pltpu.SemaphoreType.DMA,
            pltpu.SemaphoreType.DMA((6,)),
            pltpu.SemaphoreType.DMA((6,)),
        ],
        compiler_params=pltpu.CompilerParams(
            collective_id=collective_id, has_side_effects=True, vmem_limit_bytes=VMEM_BYTES
        ),
        name="scatter_rows",
    )(*([part] if old is None else [part, old]))


def dispatch_kernel(active, kept, x, *refs):
    old = refs[0] if kept else None
    out, local, send_x, recv_x, send_y, recv_y = refs[-6:]

    def run():
        me, core, cross, diag = shard_places()
        here, px, pz = expert_places()
        greet([("shard", core), ("shard", cross)] + all_owners(px, pz))
        away = {}
        for dx in range(4):
            for dz in range(4):
                if dx or dz:
                    goal = owner_at(px, pz, dx, dz)
                    at = dx * 4 + dz
                    away[at] = remote(x.at[goal], out.at[me, here], send_x.at[at], recv_x.at[at], "expert", goal)
                    away[at].start()
        own = pltpu.make_async_copy(x.at[here], out.at[me, here], local)
        own.start()
        far, near, on = [], [], []
        for dx in range(4):
            if dx == 0:
                own.wait()
            for dz in range(4):
                if dx or dz:
                    away[dx * 4 + dz].wait_recv()
            rows = pl.ds(lax.rem(px + 4 - dx, 4) * 4, 4)
            block = out.at[me, rows]
            far.append(remote(block, block, send_y.at[dx], recv_y.at[dx], "shard", cross))
            far[dx].start()
            near.append(remote(block, block, send_y.at[4 + dx], recv_y.at[4 + dx], "shard", core))
            near[dx].start()
        for dx in range(4):
            far[dx].wait_recv()
            rows = pl.ds(lax.rem(px + 4 - dx, 4) * 4, 4)
            block = out.at[cross, rows]
            on.append(remote(block, block, send_y.at[8 + dx], recv_y.at[8 + dx], "shard", core))
            on[dx].start()
        for dx in range(4):
            far[dx].wait_send()
            near[dx].wait()
            on[dx].wait()
        for at in away:
            away[at].wait_send()

    when_active(active, old, out, local, run)


def dispatch(x, old, active, collective_id):
    return pl.pallas_call(
        functools.partial(dispatch_kernel, active, old is not None),
        out_shape=jax.ShapeDtypeStruct((4, OWNERS, PIECE, HALF), jnp.bfloat16),
        in_specs=[ANY] * (1 if old is None else 2),
        out_specs=ANY,
        scratch_shapes=[
            pltpu.SemaphoreType.DMA,
            pltpu.SemaphoreType.DMA((16,)),
            pltpu.SemaphoreType.DMA((16,)),
            pltpu.SemaphoreType.DMA((12,)),
            pltpu.SemaphoreType.DMA((12,)),
        ],
        compiler_params=pltpu.CompilerParams(
            collective_id=collective_id, has_side_effects=True, vmem_limit_bytes=VMEM_BYTES
        ),
        name="dispatch",
    )(*([x] if old is None else [x, old]))


def combine_kernel(active, kept, part, *refs):
    old = refs[0] if kept else None
    out, pair, mine, theirs, crossed, total, local, send_x, recv_x, send_y, recv_y = refs[-11:]

    def run():
        me, core, cross, diag = shard_places()
        here, px, pz = expert_places()
        greet([("shard", core), ("shard", cross)] + all_owners(px, pz))
        first, second, third, away = [], [], [], {}

        def rows(dx):
            return pl.ds(lax.rem(px + dx, 4) * 4, 4)

        order = (1, 2, 3, 0)
        for n, dx in enumerate(order):
            first.append(remote(part.at[diag, rows(dx)], theirs.at[n], send_y.at[n], recv_y.at[n], "shard", core))
            first[n].start()
            second.append(
                remote(part.at[core, rows(dx)], mine.at[n], send_y.at[4 + n], recv_y.at[4 + n], "shard", core)
            )
            second[n].start()
        for n, dx in enumerate(order):
            first[n].wait_recv()
            pair[n] = (part[cross, rows(dx)].astype(jnp.float32) + theirs[n].astype(jnp.float32)).astype(jnp.bfloat16)
            third.append(remote(pair.at[n], crossed.at[n], send_y.at[8 + n], recv_y.at[8 + n], "shard", cross))
            third[n].start()
        for n, dx in enumerate(order):
            second[n].wait_recv()
            third[n].wait_recv()
            total[n] = (
                part[me, rows(dx)].astype(jnp.float32) + mine[n].astype(jnp.float32) + crossed[n].astype(jnp.float32)
            ).astype(jnp.bfloat16)
            for dz in range(4):
                goal = owner_at(px, pz, dx, dz)
                source = total.at[n, lax.rem(pz + dz, 4)]
                at = dx * 4 + dz
                if at:
                    away[at] = remote(source, out.at[here], send_x.at[at], recv_x.at[at], "expert", goal)
                else:
                    away[at] = pltpu.make_async_copy(source, out.at[here], local)
                away[at].start()
        for n in range(4):
            first[n].wait_send()
            second[n].wait_send()
            third[n].wait_send()
        for at in away:
            away[at].wait()

    when_active(active, old, out, local, run)


def combine(part, old, active, collective_id):
    return pl.pallas_call(
        functools.partial(combine_kernel, active, old is not None),
        out_shape=jax.ShapeDtypeStruct((OWNERS, PIECE, HALF), jnp.bfloat16),
        in_specs=[VMEM] + ([] if old is None else [ANY]),
        out_specs=ANY,
        scratch_shapes=[pltpu.VMEM((4, 4, PIECE, HALF), jnp.bfloat16)] * 5
        + [
            pltpu.SemaphoreType.DMA,
            pltpu.SemaphoreType.DMA((16,)),
            pltpu.SemaphoreType.DMA((16,)),
            pltpu.SemaphoreType.DMA((12,)),
            pltpu.SemaphoreType.DMA((12,)),
        ],
        compiler_params=pltpu.CompilerParams(
            collective_id=collective_id, has_side_effects=True, vmem_limit_bytes=VMEM_BYTES
        ),
        name="combine",
    )(*([part] if old is None else [part, old]))


def reduce_kernel(big, small, table, big_out, small_out, table_out, *refs):
    big_in, big_sum, pair, small_have, small_in, small_sum, table_in, local, sends, recvs, pair_send, pair_recv = refs
    me, core, cross, diag = shard_places()
    here, px, pz = expert_places()
    greet([("shard", core), ("shard", cross)] + all_owners(px, pz))
    others = [(dx * 4 + dz, owner_at(px, pz, dx, dz)) for dx in range(4) for dz in range(4) if dx or dz]
    first = []
    for at, goal in others:
        first.append(remote(big.at[goal], big_in.at[here], sends.at[0, at], recvs.at[0, at], "expert", goal))
        first[-1].start()
        first.append(remote(table, table_in.at[here], sends.at[1, at], recvs.at[1, at], "expert", goal))
        first[-1].start()
    table_in[here] = table[...]
    near = remote(small, pair.at[0], pair_send.at[0], pair_recv.at[0], "shard", core)
    near.start()
    near.wait()
    small_have[...] = small[...] + pair[0]
    far = remote(small_have, pair.at[1], pair_send.at[1], pair_recv.at[1], "shard", cross)
    far.start()
    far.wait()
    small_have[...] = small_have[...] + pair[1]
    second = []
    for at, goal in others:
        second.append(
            remote(small_have.at[goal], small_in.at[here], sends.at[2, at], recvs.at[2, at], "expert", goal)
        )
        second[-1].start()
    small_in[here] = small_have[here]
    big_in[here] = big[here]
    for copy in first:
        copy.wait()
    big_sum[...] = jnp.sum(big_in[...].astype(jnp.float32), axis=0).astype(jnp.bfloat16)
    third = []
    for at, goal in others:
        third.append(remote(big_sum, big_out.at[here], sends.at[3, at], recvs.at[3, at], "expert", goal))
        third[-1].start()
    own = pltpu.make_async_copy(big_sum, big_out.at[here], local.at[0])
    own.start()
    for copy in second:
        copy.wait()
    small_sum[...] = jnp.sum(small_in[...], axis=0)
    for at, goal in others:
        third.append(remote(small_sum, small_out.at[here], sends.at[4, at], recvs.at[4, at], "expert", goal))
        third[-1].start()
    own_small = pltpu.make_async_copy(small_sum, small_out.at[here], local.at[1])
    own_small.start()
    table_out[...] = jnp.sum(table_in[...], axis=0)
    own.wait()
    own_small.wait()
    for copy in third:
        copy.wait()


def reduce_all(big, small, table, collective_id):
    return pl.pallas_call(
        reduce_kernel,
        out_shape=(
            jax.ShapeDtypeStruct(big.shape, big.dtype),
            jax.ShapeDtypeStruct(small.shape, small.dtype),
            jax.ShapeDtypeStruct(table.shape, table.dtype),
        ),
        in_specs=[VMEM] * 3,
        out_specs=(ANY, ANY, VMEM),
        scratch_shapes=[
            pltpu.VMEM(big.shape, big.dtype),
            pltpu.VMEM(big.shape[1:], big.dtype),
            pltpu.VMEM((2,) + small.shape, small.dtype),
            pltpu.VMEM(small.shape, small.dtype),
            pltpu.VMEM(small.shape, small.dtype),
            pltpu.VMEM(small.shape[1:], small.dtype),
            pltpu.VMEM((OWNERS,) + table.shape, table.dtype),
            pltpu.SemaphoreType.DMA((2,)),
            pltpu.SemaphoreType.DMA((5, 16)),
            pltpu.SemaphoreType.DMA((5, 16)),
            pltpu.SemaphoreType.DMA((2,)),
            pltpu.SemaphoreType.DMA((2,)),
        ],
        compiler_params=pltpu.CompilerParams(
            collective_id=collective_id, has_side_effects=True, vmem_limit_bytes=VMEM_BYTES
        ),
        name="reduce_all",
    )(big, small, table)


def dot(a, b, dims=((1,), (0,))):
    return lax.dot_general(a, b, (dims, ((), ())), preferred_element_type=jnp.float32)


NT = ((1,), (1,))
TN = ((0,), (0,))


def fill_bias(by_offset, bias):
    for head in range(HEADS_HERE):
        spread = jnp.broadcast_to(by_offset[pl.ds(head, 1), :], (LEN, 2 * LEN))
        bias[head] = pltpu.roll(spread, LEN + 1, 1, stride=1, stride_axis=0)[:, :LEN]


def head_of(array, head):
    return array[:, head * HEAD_DIM : (head + 1) * HEAD_DIM]


def softmax_rows(queries, keys, bias):
    scores = dot(queries, keys, NT) * 0.125 + bias
    raised = jnp.exp(scores - jnp.max(scores, axis=1, keepdims=True))
    return raised / jnp.sum(raised, axis=1, keepdims=True)


def attend_kernel(x_ref, qkv, wo, by_offset, packed, mixed, part, bias):
    @pl.when(pl.program_id(0) == 0)
    def _():
        fill_bias(by_offset, bias)

    x = x_ref[0].reshape(LEN, D)
    q, k, v = [dot(x, qkv[which]).astype(jnp.bfloat16) for which in range(3)]
    packed[0, 0] = q
    packed[0, 1] = k
    packed[0, 2] = v
    heads = []
    for head in range(HEADS_HERE):
        chances = softmax_rows(head_of(q, head), head_of(k, head), bias[head]).astype(jnp.bfloat16)
        heads.append(dot(chances, head_of(v, head)).astype(jnp.bfloat16))
    together = jnp.concatenate(heads, axis=1)
    mixed[0] = together
    part[0] = dot(together, wo[...]).astype(jnp.bfloat16).reshape(4, ROWS, D)


def whole(shape):
    return pl.BlockSpec(shape, lambda m: (0,) * len(shape))


def per_step(shape):
    return pl.BlockSpec((1,) + shape, lambda m: (m,) + (0,) * len(shape))


WIDTH = HEADS_HERE * HEAD_DIM


def attend(normed_all, qkv_weight, out_weight, by_offset):
    return pl.pallas_call(
        attend_kernel,
        grid=(MICRO,),
        out_shape=(
            jax.ShapeDtypeStruct((MICRO, 3, LEN, WIDTH), jnp.bfloat16),
            jax.ShapeDtypeStruct((MICRO, LEN, WIDTH), jnp.bfloat16),
            jax.ShapeDtypeStruct((MICRO, 4, ROWS, D), jnp.bfloat16),
        ),
        in_specs=[per_step((4, ROWS, D)), whole((3, D, WIDTH)), whole((WIDTH, D)), whole((8, 2 * LEN))],
        out_specs=(per_step((3, LEN, WIDTH)), per_step((LEN, WIDTH)), per_step((4, ROWS, D))),
        scratch_shapes=[pltpu.VMEM((HEADS_HERE, LEN, LEN), jnp.float32)],
        compiler_params=pltpu.CompilerParams(vmem_limit_bytes=VMEM_BYTES),
        name="attend",
    )(normed_all, qkv_weight, out_weight, by_offset)


def attend_back_kernel(weighted, grad_ref, x_ref, packed, mixed, qkv, wo, by_offset, *refs):
    if weighted:
        part, weight_grad, offset_grad, bias = refs
    else:
        part, bias = refs
    number = pl.program_id(0)

    @pl.when(number == 0)
    def _():
        fill_bias(by_offset, bias)
        if weighted:
            weight_grad[...] = jnp.zeros_like(weight_grad)
            offset_grad[...] = jnp.zeros_like(offset_grad)

    grad = grad_ref[0].reshape(LEN, D)
    mixed_grad = dot(grad, wo[...], NT).astype(jnp.bfloat16)
    q, k, v = packed[0, 0], packed[0, 1], packed[0, 2]
    q_grads, k_grads, v_grads = [], [], []
    if weighted:
        row = lax.broadcasted_iota(jnp.int32, (LEN, LEN), 0)
        column = lax.broadcasted_iota(jnp.int32, (LEN, LEN), 1)
        backwards = (row + column == LEN - 1).astype(jnp.bfloat16)
    for head in range(HEADS_HERE):
        q_head, k_head, v_head = head_of(q, head), head_of(k, head), head_of(v, head)
        grad_head = head_of(mixed_grad, head)
        chances = softmax_rows(q_head, k_head, bias[head])
        grad_chances = dot(grad_head, v_head, NT)
        weighed = jnp.sum(chances * grad_chances, axis=1, keepdims=True)
        grad_scores = (chances * (grad_chances - weighed)).astype(jnp.bfloat16)
        q_grads.append((dot(grad_scores, k_head) * 0.125).astype(jnp.bfloat16))
        k_grads.append((dot(grad_scores, q_head, TN) * 0.125).astype(jnp.bfloat16))
        v_grads.append(dot(chances.astype(jnp.bfloat16), grad_head, TN).astype(jnp.bfloat16))
        if weighted:
            turned = dot(backwards, grad_scores)
            wide = jnp.concatenate([turned, jnp.zeros_like(turned)], axis=1)
            aligned = pltpu.roll(wide, 0, 1, stride=1, stride_axis=0)
            offset_grad[pl.ds(head, 1), :] += jnp.sum(aligned, axis=0, keepdims=True)
    grads = [jnp.concatenate(pieces, axis=1) for pieces in (q_grads, k_grads, v_grads)]
    summed = dot(grads[0], qkv[0], NT) + dot(grads[1], qkv[1], NT) + dot(grads[2], qkv[2], NT)
    part[0] = summed.astype(jnp.bfloat16).reshape(4, ROWS, D)
    if weighted:
        x = x_ref[0].reshape(LEN, D)
        for which in range(3):
            weight_grad[which * WIDTH : (which + 1) * WIDTH, :] += dot(grads[which], x, TN)
        weight_grad[3 * WIDTH :, :] += dot(mixed[0], grad, TN)


def attend_back(weighted, grad_all, normed_all, packed, mixed, qkv_weight, out_weight, by_offset):
    out_shape = [jax.ShapeDtypeStruct((MICRO, 4, ROWS, D), jnp.bfloat16)]
    out_specs = [per_step((4, ROWS, D))]
    if weighted:
        out_shape += [
            jax.ShapeDtypeStruct((4 * WIDTH, D), jnp.float32),
            jax.ShapeDtypeStruct((8, 2 * LEN), jnp.float32),
        ]
        out_specs += [whole((4 * WIDTH, D)), whole((8, 2 * LEN))]
    return pl.pallas_call(
        functools.partial(attend_back_kernel, weighted),
        grid=(MICRO,),
        out_shape=out_shape,
        in_specs=[
            per_step((4, ROWS, D)),
            per_step((4, ROWS, D)),
            per_step((3, LEN, WIDTH)),
            per_step((LEN, WIDTH)),
            whole((3, D, WIDTH)),
            whole((WIDTH, D)),
            whole((8, 2 * LEN)),
        ],
        out_specs=out_specs,
        scratch_shapes=[pltpu.VMEM((HEADS_HERE, LEN, LEN), jnp.float32)],
        compiler_params=pltpu.CompilerParams(vmem_limit_bytes=VMEM_BYTES),
        name="attend_back",
    )(grad_all, normed_all, packed, mixed, qkv_weight, out_weight, by_offset)


GROUPS = 8
GROUP_ROWS = 8 * PIECE
SORTED = 8 * 12


def sorting():
    order = np.zeros((2, 2 * SORTED, GROUP_ROWS), np.float32)
    for e in range(2):
        for half in range(2):
            for sender in range(8):
                for at in range(12):
                    order[e, half * SORTED + sender * 12 + at, sender * PIECE + half * 24 + e * 12 + at] = 1
    return jnp.asarray(order, jnp.bfloat16)


def sort_in(order, arrived, rows):
    for group in range(GROUPS):
        picked = dot(order, arrived[group]).astype(jnp.bfloat16)
        where = pl.ds(group * SORTED, SORTED)
        rows[where, :HALF] = picked[:SORTED]
        rows[where, HALF:] = picked[SORTED:]


def sort_out(order, rows, out, expert):
    @pl.when(expert == 0)
    def _():
        out[...] = jnp.zeros_like(out)

    for group in range(GROUPS):
        where = pl.ds(group * SORTED, SORTED)
        both = jnp.concatenate([rows[where, :HALF], rows[where, HALF:]], axis=0)
        out[group] += dot(order, both, TN).astype(jnp.bfloat16)


SCALE = 0.7978845608028654
CUBIC = 0.044715
EXPERT_ROWS = GROUPS * SORTED
TILE = 256


def experts_kernel(order, arrived, inner, outer, part, rows, results):
    sort_in(order[0], arrived, rows)

    def one_tile(number, _):
        where = pl.ds(pl.multiple_of(number * TILE, TILE), TILE)
        pre = dot(rows[where, :], inner[0])
        hidden = 0.5 * pre * (1 + jnp.tanh(SCALE * (pre + CUBIC * pre * pre * pre)))
        results[where, :] = dot(hidden.astype(jnp.bfloat16), outer[0]).astype(jnp.bfloat16)
        return 0

    lax.fori_loop(0, EXPERT_ROWS // TILE, one_tile, 0)
    sort_out(order[0], results, part, pl.program_id(0))


def experts(arrived, order, inner_weight, outer_weight):
    return pl.pallas_call(
        experts_kernel,
        grid=(2,),
        out_shape=jax.ShapeDtypeStruct((GROUPS, GROUP_ROWS, HALF), jnp.bfloat16),
        in_specs=[
            per_step((2 * SORTED, GROUP_ROWS)),
            whole((GROUPS, GROUP_ROWS, HALF)),
            per_step((D, D)),
            per_step((D, D)),
        ],
        out_specs=whole((GROUPS, GROUP_ROWS, HALF)),
        scratch_shapes=[pltpu.VMEM((EXPERT_ROWS, D), jnp.bfloat16)] * 2,
        compiler_params=pltpu.CompilerParams(vmem_limit_bytes=VMEM_BYTES),
        name="experts",
    )(order, arrived.reshape(GROUPS, GROUP_ROWS, HALF), inner_weight, outer_weight).reshape(4, OWNERS, PIECE, HALF)


def experts_back_kernel(weighted, order, arrived, grad_arrived, inner, outer, *refs):
    if weighted:
        part, inner_grad, outer_grad, rows, grads, results, hiddens, pre_grads = refs
    else:
        part, rows, grads, results = refs
    sort_in(order[0], arrived, rows)
    sort_in(order[0], grad_arrived, grads)

    def one_tile(number, _):
        where = pl.ds(pl.multiple_of(number * TILE, TILE), TILE)
        pre = dot(rows[where, :], inner[0])
        squared = pre * pre
        bent = jnp.tanh(SCALE * pre * (1 + CUBIC * squared))
        slope = 0.5 * (1 + bent) + 0.5 * pre * (1 - bent * bent) * SCALE * (1 + 3 * CUBIC * squared)
        hidden_grad = dot(grads[where, :], outer[0], NT)
        pre_grad = (hidden_grad * slope).astype(jnp.bfloat16)
        results[where, :] = dot(pre_grad, inner[0], NT).astype(jnp.bfloat16)
        if weighted:
            hiddens[where, :] = (0.5 * pre * (1 + bent)).astype(jnp.bfloat16)
            pre_grads[where, :] = pre_grad
        return 0

    lax.fori_loop(0, EXPERT_ROWS // TILE, one_tile, 0)
    sort_out(order[0], results, part, pl.program_id(0))
    if weighted:

        def one_strip(number, _):
            where = pl.ds(pl.multiple_of(number * TILE, TILE), TILE)
            inner_grad[0, where, :] = dot(rows[:, where], pre_grads[...], TN)
            outer_grad[0, where, :] = dot(hiddens[:, where], grads[...], TN)
            return 0

        lax.fori_loop(0, D // TILE, one_strip, 0)


def experts_back(weighted, arrived, grad_arrived, order, inner_weight, outer_weight):
    out_shape = [jax.ShapeDtypeStruct((GROUPS, GROUP_ROWS, HALF), jnp.bfloat16)]
    out_specs = [whole((GROUPS, GROUP_ROWS, HALF))]
    if weighted:
        out_shape += [jax.ShapeDtypeStruct((2, D, D), jnp.float32)] * 2
        out_specs += [per_step((D, D))] * 2
    results = pl.pallas_call(
        functools.partial(experts_back_kernel, weighted),
        grid=(2,),
        out_shape=out_shape,
        in_specs=[
            per_step((2 * SORTED, GROUP_ROWS)),
            whole((GROUPS, GROUP_ROWS, HALF)),
            whole((GROUPS, GROUP_ROWS, HALF)),
            per_step((D, D)),
            per_step((D, D)),
        ],
        out_specs=out_specs,
        scratch_shapes=[pltpu.VMEM((EXPERT_ROWS, D), jnp.bfloat16)] * (5 if weighted else 3),
        compiler_params=pltpu.CompilerParams(vmem_limit_bytes=VMEM_BYTES),
        name="experts_back",
    )(
        order,
        arrived.reshape(GROUPS, GROUP_ROWS, HALF),
        grad_arrived.reshape(GROUPS, GROUP_ROWS, HALF),
        inner_weight,
        outer_weight,
    )
    return (results[0].reshape(4, OWNERS, PIECE, HALF),) + tuple(results[1:])


def rms_norm(values, gain):
    return values * lax.rsqrt(jnp.mean(values * values, axis=-1, keepdims=True) + 1e-06) * gain


def bucket_of(offsets):
    distance = jnp.abs(offsets)
    far_bucket = 8 + sum(
        ((distance >= threshold).astype(jnp.int32) for threshold in (12, 16, 23, 32, 46, 64, 91))
    )
    near_far = jnp.where(distance < 8, distance, far_bucket)
    return near_far + 16 * (offsets > 0).astype(jnp.int32)


def offset_buckets():
    offsets = jnp.arange(2 * LEN, dtype=jnp.int32) - (LEN - 1)
    return (bucket_of(offsets)[:, None] == jnp.arange(32, dtype=jnp.int32)[None, :]).astype(jnp.float32)


def spread_matrix(route_ids, slot_ids):
    row = jnp.arange(OWNERS * PIECE, dtype=jnp.int32)
    part = row // 6 % 8
    half, expert, micro = part // 4, part // 2 % 2, part % 2
    row_key = ((half * 2 + micro) * EXPERTS + row // PIECE * 2 + expert) * CAP + row % 6
    block = jnp.arange(4, dtype=jnp.int32)[:, None]
    token_key = route_ids * CAP + slot_ids
    column_key = (block * (EXPERTS * CAP) + jnp.concatenate([token_key, token_key], axis=0)).reshape(-1)
    return (row_key[:, None] == column_key[None, :]).astype(jnp.bfloat16)


def to_slots(spread, rows):
    stacked = jnp.concatenate([rows[:, :HALF], rows[:, HALF:]], axis=0)
    return dot(spread, stacked).astype(jnp.bfloat16).reshape(OWNERS, PIECE, HALF)


def from_slots(spread, slots):
    stacked = dot(spread, slots.reshape(OWNERS * PIECE, HALF), TN)
    return jnp.concatenate([stacked[: MICRO * ROWS], stacked[MICRO * ROWS :]], axis=1)


def flat(rows):
    return rows.reshape(MICRO * ROWS, D)


def stack(rows):
    return rows.reshape(MICRO, ROWS, D)


def layer_forward(incoming, common, weights, old, active, first_id):
    gains, qkv_weight, out_weight, by_offset, router_weight, inner_weight, outer_weight, order = weights
    spread, chosen = common
    old = old or (None,) * 4
    residual = incoming.astype(jnp.float32)
    normed = rms_norm(residual, gains[0]).astype(jnp.bfloat16)
    normed_all = gather_rows(stack(normed), old[0], active, first_id)
    packed, mixed, part = attend(normed_all, qkv_weight, out_weight, by_offset)
    attended = scatter_rows(part, old[1], active, first_id + 1)
    middle = residual + flat(attended)
    normed_two = rms_norm(middle, gains[1]).astype(jnp.bfloat16)
    arrived = dispatch(to_slots(spread, normed_two), old[2], active, first_id + 2)
    returned = combine(experts(arrived, order, inner_weight, outer_weight), old[3], active, first_id + 3)
    logits = dot(normed_two, router_weight)
    router_prob = jax.nn.softmax(logits, axis=-1)
    gating = jnp.sum(router_prob * chosen, axis=-1)
    expert_rows = from_slots(spread, returned)
    output = (middle + gating[:, None] * expert_rows).astype(jnp.bfloat16)
    kept = (normed_all, packed, mixed, middle, normed_two, router_prob, gating, expert_rows, arrived)
    return output, kept, (normed_all, attended, arrived, returned)


def layer_backward(weighted, grad_out, incoming, common, kept, weights, old, active, first_id):
    gains, qkv_weight, out_weight, by_offset, router_weight, inner_weight, outer_weight, order = weights
    spread, chosen = common
    normed_all, packed, mixed, middle, normed_two, router_prob, gating, expert_rows, arrived = kept
    old = old or (None,) * 4
    residual = incoming.astype(jnp.float32)
    grad_expert = (gating[:, None] * grad_out).astype(jnp.bfloat16)
    grad_arrived = dispatch(to_slots(spread, grad_expert), old[0], active, first_id)
    part, *expert_grads = experts_back(weighted, arrived, grad_arrived, order, inner_weight, outer_weight)
    grad_slots = combine(part, old[1], active, first_id + 1)
    gate_grad = jnp.sum(grad_out * expert_rows, axis=-1)
    logit_grad = ((gate_grad * gating)[:, None] * (chosen - router_prob)).astype(jnp.bfloat16)
    normed_two_grad = dot(logit_grad, router_weight, NT) + from_slots(spread, grad_slots)
    _, pull_two = jax.vjp(rms_norm, middle, gains[1])
    middle_part, gain_two = pull_two(normed_two_grad)
    middle_grad = grad_out + middle_part
    grad_all = gather_rows(stack(middle_grad.astype(jnp.bfloat16)), old[2], active, first_id + 2)
    part, *attend_grads = attend_back(
        weighted, grad_all, normed_all, packed, mixed, qkv_weight, out_weight, by_offset
    )
    normed_grad = scatter_rows(part, old[3], active, first_id + 3)
    _, pull_one = jax.vjp(rms_norm, residual, gains[0])
    residual_part, gain_one = pull_one(flat(normed_grad))
    input_grad = (middle_grad + residual_part).astype(jnp.bfloat16)
    if not weighted:
        return input_grad, None, (grad_arrived, grad_slots, grad_all, normed_grad)
    router_grad = dot(logit_grad, normed_two, TN)
    return input_grad, (gain_one, gain_two, router_grad, attend_grads, expert_grads), None


def per_device(
    stream, norm_gains, attn_qkv, attn_out, rel_bias, router, expert_in, expert_out, routes, slots
):
    buckets = offset_buckets()
    by_offset = lax.dot_general(
        rel_bias[0], buckets, (((0,), (1,)), ((), ())), precision=lax.Precision.HIGHEST
    )
    by_offset = jnp.concatenate([by_offset, jnp.zeros((5, 2 * LEN), jnp.float32)], axis=0)
    weights = (
        norm_gains[0],
        attn_qkv[0],
        attn_out[0],
        by_offset,
        router[0],
        expert_in[0],
        expert_out[0],
        sorting(),
    )
    spread = spread_matrix(routes[0], slots[0])
    chosen = (routes[0].reshape(-1)[:, None] == jnp.arange(EXPERTS, dtype=jnp.int32)[None, :]).astype(jnp.float32)
    common = (spread, chosen)
    is_first = lax.axis_index("section") == 0
    own = stream[0].reshape(MICRO * ROWS, D)

    early, _, held = layer_forward(own, common, weights, None, 0, 0)
    received = lax.ppermute(early, "section", [(0, 1)])
    incoming = jnp.where(is_first, own, received)
    output, kept, _ = layer_forward(incoming, common, weights, held, 1, 4)

    grad_out = own.astype(jnp.float32)
    late, _, held = layer_backward(False, grad_out, incoming, common, kept, weights, None, 1, 8)
    returned = lax.ppermute(late, "section", [(1, 0)])
    grad_out = jnp.where(is_first, returned, own).astype(jnp.float32)
    input_grad, grads, _ = layer_backward(True, grad_out, incoming, common, kept, weights, held, 0, 12)

    gain_one, gain_two, router_grad, (attend_grad, offset_grad), (inner_grad, outer_grad) = grads
    big = attend_grad.astype(jnp.bfloat16).reshape(OWNERS, PIECE, D)
    small = jnp.concatenate([router_grad, gain_one[None], gain_two[None]], axis=0)
    small = jnp.pad(small.reshape(-1), (0, 32768 - 34 * D))
    table = jnp.dot(offset_grad[:3], buckets, precision=lax.Precision.HIGHEST)
    table = jnp.pad(table, ((0, 5), (0, 96)))
    big, small, table = reduce_all(big, small.reshape(OWNERS, 8, 256), table, 16)
    big = big.reshape(4, WIDTH, D).astype(jnp.float32)
    small = small.reshape(-1)[: 34 * D].reshape(34, D)
    end_rows = jnp.where(is_first, input_grad, output).reshape(1, MICRO, ROWS, D)
    return (
        end_rows,
        small[32:][None],
        jnp.swapaxes(big[:3], 1, 2)[None],
        big[3][None],
        table[:3, :32].T[None],
        small[:32].T[None],
        inner_grad[None],
        outer_grad[None],
    )


def solution(mesh):
    return jax.shard_map(
        per_device,
        mesh=mesh,
        in_specs=(
            P("section", None, ("expert", "shard"), None),
            P("section", None, None),
            P("section", None, None, "shard"),
            P("section", "shard", None),
            P("section", None, "shard"),
            P("section", None, None),
            P("section", "expert", None, "shard"),
            P("section", "expert", "shard", None),
            P("section", None, ("expert", "shard")),
            P("section", None, ("expert", "shard")),
        ),
        out_specs=(
            P("section", None, ("expert", "shard"), None),
            P("section", None, None),
            P("section", None, None, "shard"),
            P("section", "shard", None),
            P("section", None, "shard"),
            P("section", None, None),
            P("section", "expert", None, "shard"),
            P("section", "expert", "shard", None),
        ),
        check_vma=False,
    )
```

```python
import functools

import jax
import jax.numpy as jnp
import numpy as np
from jax import lax
from jax.experimental import pallas as pl
from jax.experimental.pallas import tpu as pltpu
from jax.sharding import PartitionSpec as P

HEAD_DIM = 64
HEADS_HERE = 3
LEN = 512
MICRO = 2
ROWS = 128
D = 768
HALF = 384
EXPERTS = 32
CAP = 6
OWNERS = 16
WAVES = 3
PIECE = 16
RELAY = False
VMEM_BYTES = 60 * 1024 * 1024
MESH = pl.DeviceIdType.MESH
ANY = pl.BlockSpec(memory_space=pl.ANY)
VMEM = pl.BlockSpec(memory_space=pltpu.VMEM)


def remote_to(src, dst, send, recv, device):
    return pltpu.make_async_remote_copy(
        src_ref=src, dst_ref=dst, send_sem=send, recv_sem=recv, device_id=device, device_id_type=MESH
    )


def remote(src, dst, send, recv, axis, index):
    return remote_to(src, dst, send, recv, {axis: index})


def greet(partners):
    barrier = pltpu.get_barrier_semaphore()
    for device in partners:
        pl.semaphore_signal(barrier, inc=1, device_id=device, device_id_type=MESH)
    return lambda: pl.semaphore_wait(barrier, len(partners))


def shard_places():
    me = lax.axis_index("shard")
    y, core = lax.div(me, 2), lax.rem(me, 2)
    return me, 2 * y + (1 - core), 2 * (1 - y) + core, 2 * (1 - y) + (1 - core)


def expert_places():
    me = lax.axis_index("expert")
    return me, lax.div(me, 4), lax.rem(me, 4)


def owner_at(x, z, dx, dz):
    return lax.rem(x + dx, 4) * 4 + lax.rem(z + dz, 4)


def all_owners(x, z):
    return [{"expert": owner_at(x, z, dx, dz)} for dx in range(4) for dz in range(4) if dx or dz]


def relays():
    other = 1 - lax.axis_index("section")
    return [{"section": other}, {"section": other, "shard": shard_places()[2]}]


class Cross:
    def __init__(self, held, sems):
        self.held = held
        self.to_send, self.to_recv, self.on_send, self.on_recv = sems
        self.ways = relays()
        self.cross = {"shard": shard_places()[2]}

    def to(self, n, half, source, goal):
        if not RELAY:
            return remote_to(source, goal, self.to_send.at[half, n], self.on_recv.at[half, n], self.cross)
        return remote_to(
            source, self.held.at[half, n], self.to_send.at[half, n], self.to_recv.at[half, n], self.ways[half]
        )

    def on(self, n, half, goal):
        return remote_to(
            self.held.at[half, n], goal, self.on_send.at[half, n], self.on_recv.at[half, n], self.ways[1 - half]
        )

    def start(self, n, sources, goals):
        for half in range(2):
            self.to(n, half, sources[half], goals[half]).start()

    def wait_recv(self, n, goals):
        for half in range(2):
            if RELAY:
                self.on(n, half, goals[half]).wait_recv()
            else:
                self.to(n, half, goals[half], goals[half]).wait_recv()

    def wait_send(self, n, sources):
        for half in range(2):
            self.to(n, half, sources[half], sources[half]).wait_send()

    def pass_on(self, n, goals):
        for half in range(2):
            self.to(n, half, goals[half], goals[half]).wait_recv()
            self.on(n, half, goals[half]).start()

    def passed(self, n, goals):
        for half in range(2):
            self.on(n, half, goals[half]).wait_send()


def across():
    return relays() if RELAY else [{"shard": shard_places()[2]}]


def when_active(active, run, rest):
    mine = lax.axis_index("section") == active
    pl.when(mine)(run)
    pl.when(jnp.logical_not(mine))(rest)


def keep_old(olds, outs, sem, between):
    keeps = [pltpu.make_async_copy(old, out, sem.at[n]) for n, (old, out) in enumerate(zip(olds, outs))]
    direct = keeps if between is None else keeps[2:]
    for keep in direct:
        keep.start()

    def done():
        for keep in direct:
            keep.wait()
        if between is not None and olds:
            for n in range(2):
                for source, goal in ((olds[n], between), (between, outs[n])):
                    hop = pltpu.make_async_copy(source, goal, sem.at[n])
                    hop.start()
                    hop.wait()

    return done


def dot(a, b, dims=((1,), (0,))):
    return lax.dot_general(a, b, (dims, ((), ())), preferred_element_type=jnp.float32)


NT = ((1,), (1,))
TN = ((0,), (0,))
WIDTH = HEADS_HERE * HEAD_DIM


def rms_norm(values, gain):
    return values * lax.rsqrt(jnp.mean(values * values, axis=-1, keepdims=True) + 1e-06) * gain


def rms_norm_back(values, gain, grad):
    scale = lax.rsqrt(jnp.mean(values * values, axis=-1, keepdims=True) + 1e-06)
    unit = values * scale
    unit_grad = grad * gain
    value_grad = scale * (unit_grad - unit * jnp.mean(unit_grad * unit, axis=-1, keepdims=True))
    return value_grad, jnp.sum(grad * unit, axis=0, keepdims=True)


def fill_bias(by_offset, bias):
    for head in range(HEADS_HERE):
        spread = jnp.broadcast_to(by_offset[pl.ds(head, 1), :], (LEN, 2 * LEN))
        bias[head] = pltpu.roll(spread, LEN + 1, 1, stride=1, stride_axis=0)[:, :LEN]


def head_of(array, head):
    return array[:, head * HEAD_DIM : (head + 1) * HEAD_DIM]


def softmax_rows(queries, keys, bias):
    scores = dot(queries, keys, NT) * 0.125 + bias
    raised = jnp.exp(scores - jnp.max(scores, axis=1, keepdims=True))
    return raised / jnp.sum(raised, axis=1, keepdims=True)


def row_halves(block):
    return [block.at[pl.ds(half * ROWS // 2, ROWS // 2)] for half in range(2)]


class Gather:
    def __init__(self, rows, held, sems):
        self.rows, self.send, self.recv = rows, sems[0], sems[1]
        self.cross_link = Cross(held, sems[2:])
        self.me, self.core, self.cross, _ = shard_places()

    def piece(self, m, whose, kind):
        block = self.rows.at[m, whose]
        at = 2 * kind + m
        return remote(block, block, self.send.at[at], self.recv.at[at], "shard", self.core)

    def start(self, m):
        block = row_halves(self.rows.at[m, self.me])
        self.cross_link.start(m, block, block)
        self.near(m).start()

    def near(self, m):
        return self.piece(m, self.me, 0)

    def on(self, m):
        return self.piece(m, self.cross, 1)

    def hand_on(self, m):
        self.cross_link.wait_recv(m, row_halves(self.rows.at[m, self.cross]))
        self.on(m).start()

    def finish(self, m):
        self.near(m).wait_recv()
        self.on(m).wait_recv()

    def drain(self):
        for m in range(MICRO):
            self.cross_link.wait_send(m, row_halves(self.rows.at[m, self.me]))
            self.near(m).wait_send()
            self.on(m).wait_send()

    def goals(self, m):
        return [row_halves(self.rows.at[m, whose])[half] for half, whose in enumerate((self.me, self.cross))]

    def pass_on(self):
        for m in range(MICRO):
            self.cross_link.pass_on(m, self.goals(m))

    def passed(self):
        for m in range(MICRO):
            self.cross_link.passed(m, self.goals(m))


class HeadSum:
    def __init__(self, part, buffers, held, sems):
        self.part, self.send, self.recv = part, sems[0], sems[1]
        self.cross_link = Cross(held, sems[2:])
        self.pair, self.mine, self.theirs, self.crossed = buffers
        self.me, self.core, self.cross, self.diag = shard_places()

    def first(self, m):
        return remote(self.part.at[m, self.diag], self.theirs.at[m], self.send.at[m], self.recv.at[m], "shard", self.core)

    def second(self, m):
        return remote(
            self.part.at[m, self.core], self.mine.at[m], self.send.at[2 + m], self.recv.at[2 + m], "shard", self.core
        )

    def start(self, m):
        self.first(m).start()
        self.second(m).start()

    def cross_over(self, m):
        self.first(m).wait_recv()
        self.pair[m] = (self.part[m, self.cross].astype(jnp.float32) + self.theirs[m].astype(jnp.float32)).astype(
            jnp.bfloat16
        )
        self.cross_link.start(m, row_halves(self.pair.at[m]), row_halves(self.crossed.at[m]))

    def total(self, m):
        self.second(m).wait_recv()
        self.cross_link.wait_recv(m, row_halves(self.crossed.at[m]))
        return (
            self.part[m, self.me].astype(jnp.float32)
            + self.mine[m].astype(jnp.float32)
            + self.crossed[m].astype(jnp.float32)
        )

    def drain(self):
        for m in range(MICRO):
            self.first(m).wait_send()
            self.second(m).wait_send()
            self.cross_link.wait_send(m, row_halves(self.pair.at[m]))

    def pass_on(self):
        for m in range(MICRO):
            self.cross_link.pass_on(m, row_halves(self.crossed.at[m]))

    def passed(self):
        for m in range(MICRO):
            self.cross_link.passed(m, row_halves(self.crossed.at[m]))


SHARD_BUFFERS = (
    [pltpu.VMEM((MICRO, 4, ROWS, D), jnp.bfloat16)]
    + [pltpu.VMEM((MICRO, ROWS, D), jnp.bfloat16)] * 4
    + [pltpu.VMEM((2, MICRO, ROWS // 2, D), jnp.bfloat16)] * 2
)
SHARD_SEMS = ([pltpu.SemaphoreType.DMA((4,))] * 2 + [pltpu.SemaphoreType.DMA((2, MICRO))] * 4) * 2


def shard_group(gathered, buffers, sems):
    part, pair, mine, theirs, crossed, held, held_sum = buffers
    gather = Gather(gathered, held, sems[:6])
    heads_sum = HeadSum(part, (pair, mine, theirs, crossed), held_sum, sems[6:])
    return gather, heads_sum, part


def attend(rows, gains, qkv, wo, by_offset, outs, bias, gather, heads_sum, part):
    normed_all, packed, mixed, middle = outs
    fill_bias(by_offset, bias)
    for m in range(MICRO):
        gather.hand_on(m)
    for m in range(MICRO):
        gather.finish(m)
        x = normed_all[m].reshape(LEN, D)
        q, k, v = [dot(x, qkv[which]).astype(jnp.bfloat16) for which in range(3)]
        packed[m, 0] = q
        packed[m, 1] = k
        packed[m, 2] = v
        if m:
            heads_sum.cross_over(m - 1)
        heads = []
        for head in range(HEADS_HERE):
            chances = softmax_rows(head_of(q, head), head_of(k, head), bias[head]).astype(jnp.bfloat16)
            heads.append(dot(chances, head_of(v, head)).astype(jnp.bfloat16))
        together = jnp.concatenate(heads, axis=1)
        mixed[m] = together
        part[m] = dot(together, wo[...]).astype(jnp.bfloat16).reshape(4, ROWS, D)
        heads_sum.start(m)
    heads_sum.cross_over(MICRO - 1)
    for m in range(MICRO):
        middle[m] = rows[m].astype(jnp.float32) + heads_sum.total(m)


def attend_back(
    middle_grad, rows, gains, normed_all, packed, mixed, qkv, wo, by_offset, outs, grad_all, dqkv, bias, gather, heads_sum, part
):
    input_grad, weight_grad, offset_grad, gain_grad = outs
    me = shard_places()[0]
    for m in range(MICRO):
        grad_all[m, me] = middle_grad[m].astype(jnp.bfloat16)
        gather.start(m)
    offset_grad[...] = jnp.zeros_like(offset_grad)
    row = lax.broadcasted_iota(jnp.int32, (LEN, LEN), 0)
    column = lax.broadcasted_iota(jnp.int32, (LEN, LEN), 1)
    backwards = (row + column == LEN - 1).astype(jnp.bfloat16)
    for m in range(MICRO):
        gather.hand_on(m)
    for m in range(MICRO):
        gather.finish(m)
        grad = grad_all[m].reshape(LEN, D)
        mixed_grad = dot(grad, wo[...], NT).astype(jnp.bfloat16)
        if m:
            heads_sum.cross_over(m - 1)
        q, k, v = packed[m, 0], packed[m, 1], packed[m, 2]
        q_grads, k_grads, v_grads = [], [], []
        for head in range(HEADS_HERE):
            q_head, k_head, v_head = head_of(q, head), head_of(k, head), head_of(v, head)
            grad_head = head_of(mixed_grad, head)
            chances = softmax_rows(q_head, k_head, bias[head])
            grad_chances = dot(grad_head, v_head, NT)
            weighed = jnp.sum(chances * grad_chances, axis=1, keepdims=True)
            grad_scores = (chances * (grad_chances - weighed)).astype(jnp.bfloat16)
            q_grads.append((dot(grad_scores, k_head) * 0.125).astype(jnp.bfloat16))
            k_grads.append((dot(grad_scores, q_head, TN) * 0.125).astype(jnp.bfloat16))
            v_grads.append(dot(chances.astype(jnp.bfloat16), grad_head, TN).astype(jnp.bfloat16))
            turned = dot(backwards, grad_scores)
            wide = jnp.concatenate([turned, jnp.zeros_like(turned)], axis=1)
            aligned = pltpu.roll(wide, 0, 1, stride=1, stride_axis=0)
            offset_grad[pl.ds(head, 1), :] += jnp.sum(aligned, axis=0, keepdims=True)
        grads = [jnp.concatenate(pieces, axis=1) for pieces in (q_grads, k_grads, v_grads)]
        for which in range(3):
            dqkv[m, which] = grads[which]
        summed = dot(grads[0], qkv[0], NT) + dot(grads[1], qkv[1], NT) + dot(grads[2], qkv[2], NT)
        part[m] = summed.astype(jnp.bfloat16).reshape(4, ROWS, D)
        heads_sum.start(m)
        if m:
            heads_sum.cross_over(m)
        x = normed_all[m].reshape(LEN, D)
        for which in range(4):
            left = dqkv[m, which] if which < 3 else mixed[m]
            added = dot(left, x if which < 3 else grad, TN)
            where = pl.ds(which * WIDTH, WIDTH)
            weight_grad[where, :] = added if m == 0 else weight_grad[where, :] + added
    gain_total = jnp.zeros((1, D), jnp.float32)
    for m in range(MICRO):
        back, gain_part = rms_norm_back(rows[m].astype(jnp.float32), gains[0:1, :], heads_sum.total(m))
        input_grad[m] = (middle_grad[m] + back).astype(jnp.bfloat16)
        gain_total = gain_total + gain_part
    gain_grad[...] = jnp.broadcast_to(gain_total, (8, D))


GROUP_ROWS = 16 * PIECE
SORTED = 16 * 4
WAVE_ROWS = 4 * SORTED
PAIRS = [(dx, dz) for dx in range(4) for dz in range(4) if dx or dz]


def sorting():
    order = np.zeros((GROUP_ROWS, GROUP_ROWS), np.float32)
    for e in range(2):
        for half in range(2):
            for sender in range(16):
                for at in range(4):
                    order[(e * 2 + half) * SORTED + sender * 4 + at, sender * PIECE + half * 8 + e * 4 + at] = 1
    return jnp.asarray(order, jnp.bfloat16), jnp.asarray(order.T, jnp.bfloat16)


def sender_halves(block):
    return [block.at[pl.ds(8 * half, 8)] for half in range(2)]


class SlotsOut:
    def __init__(self, slots, arrived, held, sems):
        self.slots, self.arrived = slots, arrived
        self.send_x, self.recv_x, self.send_y, self.recv_y = sems[:4]
        self.cross_link = Cross(held, sems[4:])
        self.me, self.core, self.cross, _ = shard_places()
        self.here, self.px, self.pz = expert_places()

    def away(self, w, dx, dz):
        at = w * 16 + dx * 4 + dz
        goal = owner_at(self.px, self.pz, dx, dz)
        return remote(
            self.slots.at[w, goal],
            self.arrived.at[self.me, w, self.here],
            self.send_x.at[at],
            self.recv_x.at[at],
            "expert",
            goal,
        )

    def piece(self, w, whose, kind):
        block = self.arrived.at[whose, w]
        at = WAVES * kind + w
        return remote(block, block, self.send_y.at[at], self.recv_y.at[at], "shard", self.core)

    def near(self, w):
        return self.piece(w, self.me, 0)

    def on(self, w):
        return self.piece(w, self.cross, 1)

    def start(self, w):
        for dx, dz in PAIRS:
            self.away(w, dx, dz).start()
        self.arrived[self.me, w, self.here] = self.slots[w, self.here]

    def sent(self, w):
        for dx, dz in PAIRS:
            self.away(w, dx, dz).wait_send()

    def spread_on(self, w):
        for dx, dz in PAIRS:
            self.away(w, dx, dz).wait_recv()
        block = sender_halves(self.arrived.at[self.me, w])
        self.cross_link.start(w, block, block)
        self.near(w).start()

    def hand_on(self, w):
        self.cross_link.wait_recv(w, sender_halves(self.arrived.at[self.cross, w]))
        self.on(w).start()

    def finish(self, w):
        self.near(w).wait_recv()
        self.on(w).wait_recv()

    def drain(self):
        for w in range(WAVES):
            self.cross_link.wait_send(w, sender_halves(self.arrived.at[self.me, w]))
            self.near(w).wait_send()
            self.on(w).wait_send()

    def goals(self, w):
        return [sender_halves(self.arrived.at[whose, w])[half] for half, whose in enumerate((self.me, self.cross))]

    def pass_on(self):
        for w in range(WAVES):
            self.cross_link.pass_on(w, self.goals(w))

    def passed(self):
        for w in range(WAVES):
            self.cross_link.passed(w, self.goals(w))


class SlotsBack:
    def __init__(self, part, returned, buffers, held, sems):
        self.part, self.returned = part, returned
        self.pair, self.mine, self.theirs, self.crossed, self.total = buffers
        self.send_x, self.recv_x, self.send_y, self.recv_y = sems[:4]
        self.cross_link = Cross(held, sems[4:])
        self.me, self.core, self.cross, self.diag = shard_places()
        self.here, self.px, self.pz = expert_places()

    def to_core(self, w, whose, buffer, kind):
        at = WAVES * kind + w
        return remote(self.part.at[whose, w], buffer.at[w], self.send_y.at[at], self.recv_y.at[at], "shard", self.core)

    def first(self, w):
        return self.to_core(w, self.diag, self.theirs, 0)

    def second(self, w):
        return self.to_core(w, self.core, self.mine, 1)

    def away(self, w, dx, dz):
        at = w * 16 + dx * 4 + dz
        goal = owner_at(self.px, self.pz, dx, dz)
        return remote(
            self.total.at[w, goal],
            self.returned.at[w, self.here],
            self.send_x.at[at],
            self.recv_x.at[at],
            "expert",
            goal,
        )

    def start(self, w):
        self.first(w).start()
        self.second(w).start()

    def cross_over(self, w):
        self.first(w).wait_recv()
        self.pair[w] = (self.part[self.cross, w].astype(jnp.float32) + self.theirs[w].astype(jnp.float32)).astype(
            jnp.bfloat16
        )
        self.cross_link.start(w, sender_halves(self.pair.at[w]), sender_halves(self.crossed.at[w]))

    def send_home(self, w):
        self.second(w).wait_recv()
        self.cross_link.wait_recv(w, sender_halves(self.crossed.at[w]))
        self.total[w] = (
            self.part[self.me, w].astype(jnp.float32)
            + self.mine[w].astype(jnp.float32)
            + self.crossed[w].astype(jnp.float32)
        ).astype(jnp.bfloat16)
        for dx, dz in PAIRS:
            self.away(w, dx, dz).start()
        self.returned[w, self.here] = self.total[w, self.here]

    def finish(self):
        for w in range(WAVES):
            for dx, dz in PAIRS:
                self.away(w, dx, dz).wait_recv()

    def drain(self):
        for w in range(WAVES):
            self.first(w).wait_send()
            self.second(w).wait_send()
            self.cross_link.wait_send(w, sender_halves(self.pair.at[w]))
            for dx, dz in PAIRS:
                self.away(w, dx, dz).wait_send()

    def pass_on(self):
        for w in range(WAVES):
            self.cross_link.pass_on(w, sender_halves(self.crossed.at[w]))

    def passed(self):
        for w in range(WAVES):
            self.cross_link.passed(w, sender_halves(self.crossed.at[w]))


def to_slots(spread, rows, slots):
    stacked = jnp.concatenate([rows[:, :HALF], rows[:, HALF:]], axis=0)
    slots[...] = dot(spread, stacked).astype(jnp.bfloat16).reshape(WAVES, OWNERS, PIECE, HALF)


def from_slots(spread_t, slots):
    stacked = dot(spread_t, slots[...].reshape(WAVES * OWNERS * PIECE, HALF))
    return jnp.concatenate([stacked[: MICRO * ROWS], stacked[MICRO * ROWS :]], axis=1)


def sort_in(order, arrived, w, rows, base):
    for group in range(4):
        picked = dot(order, arrived[group, w].reshape(GROUP_ROWS, HALF)).astype(jnp.bfloat16)
        for e in range(2):
            for half in range(2):
                at = (2 * e + half) * SORTED
                rows[e, pl.ds(base + group * SORTED, SORTED), half * HALF : (half + 1) * HALF] = picked[at : at + SORTED]


def sort_out(order_t, results, part, w):
    for group in range(4):
        where = slice(group * SORTED, (group + 1) * SORTED)
        pieces = [results[e, where, half * HALF : (half + 1) * HALF] for e in range(2) for half in range(2)]
        block = dot(order_t, jnp.concatenate(pieces, axis=0)).astype(jnp.bfloat16)
        part[group, w] = block.reshape(OWNERS, PIECE, HALF)


SCALE = 0.7978845608028654
CUBIC = 0.044715


def flat(rows):
    return rows.reshape(MICRO * ROWS, D)


SLOT_SEMS = (
    [pltpu.SemaphoreType.DMA((16 * WAVES,))] * 2
    + [pltpu.SemaphoreType.DMA((2 * WAVES,))] * 2
    + [pltpu.SemaphoreType.DMA((2, WAVES))] * 4
) * 2
SLOT_BUFFERS = (
    [pltpu.VMEM((WAVES, OWNERS, PIECE, HALF), jnp.bfloat16)] * 2
    + [pltpu.VMEM((4, WAVES, OWNERS, PIECE, HALF), jnp.bfloat16)]
    + [pltpu.VMEM((WAVES, OWNERS, PIECE, HALF), jnp.bfloat16)] * 5
    + [pltpu.VMEM((2, WAVES, 8, PIECE, HALF), jnp.bfloat16)] * 2
)


def slot_exchange(arrived, buffers, sems):
    slots, returned, part, pair, mine, theirs, crossed, total, held_out, held_back = buffers
    out = SlotsOut(slots, arrived, held_out, sems[:8])
    back = SlotsBack(part, returned, (pair, mine, theirs, crossed, total), held_back, sems[8:])
    return out, back


def pipeline(out, back, beside, compute):
    out.start(0)
    beside()
    out.sent(0)
    out.start(1)
    out.spread_on(0)
    out.sent(1)
    out.start(2)
    out.spread_on(1)
    out.hand_on(0)
    out.sent(2)
    out.spread_on(2)
    out.hand_on(1)
    out.finish(0)
    compute(0)
    back.start(0)
    out.hand_on(2)
    out.finish(1)
    back.cross_over(0)
    compute(1)
    back.start(1)
    out.finish(2)
    back.cross_over(1)
    back.send_home(0)
    compute(2)
    back.start(2)
    back.send_home(1)
    back.cross_over(2)


def experts(middle, gains, router, spread, spread_t, chosen, order, order_t, inner, outer, fetched, outs, arrived, results, out, back):
    rows, normed_two, router_prob, gating, expert_rows, output = outs
    normed = rms_norm(flat(middle[...]), gains[1:2, :]).astype(jnp.bfloat16)
    normed_two[...] = normed
    to_slots(spread[...], normed, out.slots)

    def beside():
        logits = dot(normed, router[...])
        raised = jnp.exp(logits - jnp.max(logits, axis=1, keepdims=True))
        prob = raised / jnp.sum(raised, axis=1, keepdims=True)
        router_prob[...] = prob
        gating[...] = jnp.sum(prob * chosen[...], axis=1, keepdims=True)
        fetched()

    def compute(w):
        sort_in(order[...], arrived, w, rows, w * WAVE_ROWS)

        def one_expert(e, _):
            pre = dot(rows[e, pl.ds(w * WAVE_ROWS, WAVE_ROWS), :], inner[e])
            hidden = 0.5 * pre * (1 + jnp.tanh(SCALE * (pre + CUBIC * pre * pre * pre)))
            results[e] = dot(hidden.astype(jnp.bfloat16), outer[e]).astype(jnp.bfloat16)
            return 0

        lax.fori_loop(0, 2, one_expert, 0)
        sort_out(order_t[...], results, back.part, w)

    pipeline(out, back, beside, compute)
    back.send_home(WAVES - 1)
    back.finish()
    found = from_slots(spread_t[...], back.returned)
    expert_rows[...] = found.astype(jnp.bfloat16)
    output[...] = (flat(middle[...]) + gating[...] * found).astype(jnp.bfloat16).reshape(MICRO, ROWS, D)


def experts_back(
    grad_out,
    middle,
    normed_two,
    router_prob,
    gating,
    expert_rows,
    gains,
    router,
    spread,
    spread_t,
    chosen,
    order,
    order_t,
    inner,
    outer,
    fetched,
    outs,
    middle_grad,
    grad_arrived,
    scratch,
    local,
    out,
    back,
):
    inner_grad, outer_grad, router_grad, gain_grad = outs
    rows, grads, hiddens, pre_grads, results, held = scratch
    grad = flat(grad_out[...]).astype(jnp.float32)
    to_slots(spread[...], (gating[...] * grad).astype(jnp.bfloat16), out.slots)
    gate_grad = jnp.sum(grad * expert_rows[...].astype(jnp.float32), axis=1, keepdims=True)
    logit_grad = ((gate_grad * gating[...]) * (chosen[...] - router_prob[...])).astype(jnp.bfloat16)

    def beside():
        router_grad[...] = dot(logit_grad, normed_two[...], TN)
        fetched()

    def compute(w):
        base = w * WAVE_ROWS
        where = pl.ds(base, WAVE_ROWS)
        sort_in(order[...], grad_arrived, w, grads, base)

        def one_expert(e, _):
            pre = dot(rows[e, where, :], inner[e])
            squared = pre * pre
            bent = jnp.tanh(SCALE * pre * (1 + CUBIC * squared))
            slope = 0.5 * (1 + bent) + 0.5 * pre * (1 - bent * bent) * SCALE * (1 + 3 * CUBIC * squared)
            hiddens[e, where, :] = (0.5 * pre * (1 + bent)).astype(jnp.bfloat16)
            pre_grad = (dot(grads[e, where, :], outer[e], NT) * slope).astype(jnp.bfloat16)
            pre_grads[e, where, :] = pre_grad
            results[e] = dot(pre_grad, inner[e], NT).astype(jnp.bfloat16)
            return 0

        lax.fori_loop(0, 2, one_expert, 0)
        sort_out(order_t[...], results, back.part, w)

    writes = []

    def weight_grads(number, left, right, goal):
        if number:
            writes.pop().wait()

        def one_expert(e, _):
            for at in range(0, D, 256):
                held[e, at : at + 256, :] = dot(left[e, :, at : at + 256], right[e], TN)
            return 0

        lax.fori_loop(0, 2, one_expert, 0)
        write = pltpu.make_async_copy(held, goal, local.at[number])
        write.start()
        writes.append(write)

    pipeline(out, back, beside, compute)
    weight_grads(0, rows, pre_grads, inner_grad)
    back.send_home(WAVES - 1)
    weight_grads(1, hiddens, grads, outer_grad)
    back.finish()
    normed_grad = dot(logit_grad, router[...], NT) + from_slots(spread_t[...], back.returned)
    value_grad, gain_part = rms_norm_back(flat(middle[...]), gains[1:2, :], normed_grad)
    middle_grad[...] = (grad + value_grad).reshape(MICRO, ROWS, D)
    gain_grad[...] = jnp.broadcast_to(gain_part, (8, D))
    return writes


def fetch(pairs, sems, first):
    copies = [pltpu.make_async_copy(source, goal, sems.at[first + n]) for n, (source, goal) in enumerate(pairs)]
    for copy in copies:
        copy.start()

    def fetched():
        for copy in copies:
            copy.wait()

    return fetched


def over_section(source, goal, sems, m):
    other = 1 - lax.axis_index("section")
    return remote(source.at[m], goal.at[m], sems.at[0, m], sems.at[1, m], "section", other)


def greet_active(moved):
    _, px, pz = expert_places()
    core = [{"shard": shard_places()[1]}]
    peer = [] if RELAY or not moved else [{"section": 1 - lax.axis_index("section")}]
    return greet(core + across() + peer + all_owners(px, pz))


def greet_idle(moved):
    if RELAY:
        greet(relays())()
    elif moved:
        greet([{"section": 1 - lax.axis_index("section")}])()


def hand_over(stages):
    if RELAY:
        for stage in stages:
            stage.pass_on()
        for stage in stages:
            stage.passed()


SECTION_SEM = pltpu.SemaphoreType.DMA((2, MICRO))
LOCAL_SEM = pltpu.SemaphoreType.DMA((12,))
ARRIVED = pltpu.VMEM((4, WAVES, OWNERS, PIECE, HALF), jnp.bfloat16)
WEIGHTS = [pltpu.VMEM((2, D, D), jnp.bfloat16)] * 2
FORWARD_OUTS = (
    jax.ShapeDtypeStruct((MICRO, 4, ROWS, D), jnp.bfloat16),
    jax.ShapeDtypeStruct((MICRO, 3, LEN, WIDTH), jnp.bfloat16),
    jax.ShapeDtypeStruct((MICRO, LEN, WIDTH), jnp.bfloat16),
    jax.ShapeDtypeStruct((MICRO, ROWS, D), jnp.float32),
    jax.ShapeDtypeStruct((2, WAVES * WAVE_ROWS, D), jnp.bfloat16),
    jax.ShapeDtypeStruct((MICRO * ROWS, D), jnp.bfloat16),
    jax.ShapeDtypeStruct((MICRO * ROWS, EXPERTS), jnp.float32),
    jax.ShapeDtypeStruct((MICRO * ROWS, 1), jnp.float32),
    jax.ShapeDtypeStruct((MICRO * ROWS, D), jnp.bfloat16),
    jax.ShapeDtypeStruct((MICRO, ROWS, D), jnp.bfloat16),
)


def forward_kernel(active, kept, own, gains, qkv, wo, by_offset, router, spread, spread_t, chosen, order, order_t, inner, outer, *refs):
    olds, refs = refs[: 10 * kept], refs[10 * kept :]
    outs, refs = refs[:10], refs[10:]
    received, refs = refs[:kept], refs[kept:]
    bias, inner_here, outer_here, arrived, results, section, local = refs[:7]
    shard_buffers, slot_buffers, shard_sems, slot_sems = refs[7:14], refs[14:24], refs[24:36], refs[36:]
    gather, heads_sum, part = shard_group(outs[0], shard_buffers, shard_sems)
    out, back = slot_exchange(arrived, slot_buffers, slot_sems)
    incoming = received[0] if kept else own

    def run():
        ready = greet_active(kept)
        fetched = fetch([(inner, inner_here), (outer, outer_here)], local, 0)
        ready()
        me = shard_places()[0]
        for m in range(MICRO):
            if kept:
                over_section(olds[9], incoming, section, m).wait_recv()
            outs[0][m, me] = rms_norm(incoming[m].astype(jnp.float32), gains[0:1, :]).astype(jnp.bfloat16)
            gather.start(m)
        attend(incoming, gains, qkv, wo, by_offset, outs[:4], bias, gather, heads_sum, part)
        routing = (gains, router, spread, spread_t, chosen, order, order_t, inner_here, outer_here)
        experts(outs[3], *routing, fetched, outs[4:], arrived, results, out, back)
        for stage in (gather, heads_sum, out, back):
            stage.drain()

    def rest():
        done = keep_old(olds[:9], outs[:9], local, None)
        greet_idle(kept)
        if kept:
            for m in range(MICRO):
                over_section(olds[9], incoming, section, m).start()
            incoming[...] = own[...]
        hand_over((gather, heads_sum, out, back))
        if kept:
            for m in range(MICRO):
                over_section(olds[9], incoming, section, m).wait_send()
        done()

    when_active(active, run, rest)


def layer_forward(own, common, olds, active, collective_id):
    kept = olds is not None
    return pl.pallas_call(
        functools.partial(forward_kernel, active, int(kept)),
        out_shape=FORWARD_OUTS + ((jax.ShapeDtypeStruct((MICRO, ROWS, D), jnp.bfloat16),) if kept else ()),
        in_specs=[VMEM] * 11 + [ANY] * (12 if kept else 2),
        out_specs=(VMEM,) * (11 if kept else 10),
        scratch_shapes=[pltpu.VMEM((HEADS_HERE, LEN, LEN), jnp.float32)]
        + WEIGHTS
        + [ARRIVED, pltpu.VMEM((2, WAVE_ROWS, D), jnp.bfloat16), SECTION_SEM, LOCAL_SEM]
        + SHARD_BUFFERS
        + SLOT_BUFFERS
        + SHARD_SEMS
        + SLOT_SEMS,
        compiler_params=pltpu.CompilerParams(
            collective_id=collective_id, has_side_effects=True, vmem_limit_bytes=VMEM_BYTES
        ),
        name="layer_forward",
    )(own, *common, *(olds or ()))


BACKWARD_OUTS = (
    jax.ShapeDtypeStruct((2, D, D), jnp.float32),
    jax.ShapeDtypeStruct((2, D, D), jnp.float32),
    jax.ShapeDtypeStruct((EXPERTS, D), jnp.float32),
    jax.ShapeDtypeStruct((8, D), jnp.float32),
    jax.ShapeDtypeStruct((4 * WIDTH, D), jnp.float32),
    jax.ShapeDtypeStruct((8, 2 * LEN), jnp.float32),
    jax.ShapeDtypeStruct((8, D), jnp.float32),
    jax.ShapeDtypeStruct((MICRO, ROWS, D), jnp.bfloat16),
)


def backward_kernel(
    active,
    kept,
    own,
    gains,
    qkv,
    wo,
    by_offset,
    router,
    spread,
    spread_t,
    chosen,
    order,
    order_t,
    inner,
    outer,
    normed_all,
    packed,
    mixed,
    middle,
    saved_rows,
    normed_two,
    router_prob,
    gating,
    expert_rows,
    incoming,
    *refs,
):
    olds, refs = refs[: 8 * kept], refs[8 * kept :]
    outs, refs = refs[:8], refs[8:]
    received, middle_grad, grad_arrived, grad_all, dqkv, bias, inner_here, outer_here, section, local = refs[:10]
    scratch, shard_buffers, slot_buffers = refs[10:16], refs[16:23], refs[23:33]
    shard_sems, slot_sems = refs[33:45], refs[45:]
    gather, heads_sum, part = shard_group(grad_all, shard_buffers, shard_sems)
    out, back = slot_exchange(grad_arrived, slot_buffers, slot_sems)
    grad_out = received if kept else own

    def run():
        ready = greet_active(kept)
        fetched = fetch([(inner, inner_here), (outer, outer_here), (saved_rows, scratch[0])], local, 2)
        fill_bias(by_offset, bias)
        ready()
        if kept:
            for m in range(MICRO):
                over_section(olds[7], grad_out, section, m).wait_recv()
        writes = experts_back(
            grad_out,
            middle,
            normed_two,
            router_prob,
            gating,
            expert_rows,
            gains,
            router,
            spread,
            spread_t,
            chosen,
            order,
            order_t,
            inner_here,
            outer_here,
            fetched,
            outs[:4],
            middle_grad,
            grad_arrived,
            scratch,
            local,
            out,
            back,
        )
        attend_back(
            middle_grad,
            incoming,
            gains,
            normed_all,
            packed,
            mixed,
            qkv,
            wo,
            by_offset,
            (outs[7], outs[4], outs[5], outs[6]),
            grad_all,
            dqkv,
            bias,
            gather,
            heads_sum,
            part,
        )
        for stage in (out, back, gather, heads_sum):
            stage.drain()
        for write in writes:
            write.wait()

    def rest():
        done = keep_old(olds[:7], outs[:7], local, scratch[5])
        greet_idle(kept)
        if kept:
            for m in range(MICRO):
                over_section(olds[7], grad_out, section, m).start()
        hand_over((out, back, gather, heads_sum))
        if kept:
            for m in range(MICRO):
                over_section(olds[7], grad_out, section, m).wait_send()
        done()

    when_active(active, run, rest)


def layer_backward(own, common, saved, olds, active, collective_id):
    kept = olds is not None
    all_rows = pltpu.VMEM((2, WAVES * WAVE_ROWS, D), jnp.bfloat16)
    return pl.pallas_call(
        functools.partial(backward_kernel, active, int(kept)),
        out_shape=BACKWARD_OUTS,
        in_specs=[VMEM] * 11 + [ANY] * 2 + [VMEM] * 4 + [ANY] + [VMEM] * 5 + [ANY] * (8 if kept else 0),
        out_specs=(ANY, ANY) + (VMEM,) * 6,
        scratch_shapes=[
            pltpu.VMEM((MICRO, ROWS, D), jnp.bfloat16),
            pltpu.VMEM((MICRO, ROWS, D), jnp.float32),
            ARRIVED,
            pltpu.VMEM((MICRO, 4, ROWS, D), jnp.bfloat16),
            pltpu.VMEM((MICRO, 3, LEN, WIDTH), jnp.bfloat16),
            pltpu.VMEM((HEADS_HERE, LEN, LEN), jnp.float32),
        ]
        + WEIGHTS
        + [SECTION_SEM, LOCAL_SEM]
        + [all_rows] * 4
        + [pltpu.VMEM((2, WAVE_ROWS, D), jnp.bfloat16), pltpu.VMEM((2, D, D), jnp.float32)]
        + SHARD_BUFFERS
        + SLOT_BUFFERS
        + SHARD_SEMS
        + SLOT_SEMS,
        compiler_params=pltpu.CompilerParams(
            collective_id=collective_id, has_side_effects=True, vmem_limit_bytes=VMEM_BYTES
        ),
        name="layer_backward",
    )(own, *common, *saved, *(olds or ()))


def reduce_kernel(big, small, table, big_out, small_out, table_out, *refs):
    big_in, big_sum, pair, small_have, small_in, small_sum, table_in, local, sends, recvs, pair_send, pair_recv = refs
    me, core, cross, diag = shard_places()
    here, px, pz = expert_places()
    greet([{"shard": core}, {"shard": cross}] + all_owners(px, pz))()
    others = [(dx * 4 + dz, owner_at(px, pz, dx, dz)) for dx in range(4) for dz in range(4) if dx or dz]
    first = []
    for at, goal in others:
        first.append(remote(big.at[goal], big_in.at[here], sends.at[0, at], recvs.at[0, at], "expert", goal))
        first[-1].start()
        first.append(remote(table, table_in.at[here], sends.at[1, at], recvs.at[1, at], "expert", goal))
        first[-1].start()
    table_in[here] = table[...]
    near = remote(small, pair.at[0], pair_send.at[0], pair_recv.at[0], "shard", core)
    near.start()
    near.wait()
    small_have[...] = small[...] + pair[0]
    far = remote(small_have, pair.at[1], pair_send.at[1], pair_recv.at[1], "shard", cross)
    far.start()
    far.wait()
    small_have[...] = small_have[...] + pair[1]
    second = []
    for at, goal in others:
        second.append(
            remote(small_have.at[goal], small_in.at[here], sends.at[2, at], recvs.at[2, at], "expert", goal)
        )
        second[-1].start()
    small_in[here] = small_have[here]
    big_in[here] = big[here]
    for copy in first:
        copy.wait()
    big_sum[...] = jnp.sum(big_in[...].astype(jnp.float32), axis=0).astype(jnp.bfloat16)
    third = []
    for at, goal in others:
        third.append(remote(big_sum, big_out.at[here], sends.at[3, at], recvs.at[3, at], "expert", goal))
        third[-1].start()
    own = pltpu.make_async_copy(big_sum, big_out.at[here], local.at[0])
    own.start()
    for copy in second:
        copy.wait()
    small_sum[...] = jnp.sum(small_in[...], axis=0)
    for at, goal in others:
        third.append(remote(small_sum, small_out.at[here], sends.at[4, at], recvs.at[4, at], "expert", goal))
        third[-1].start()
    own_small = pltpu.make_async_copy(small_sum, small_out.at[here], local.at[1])
    own_small.start()
    table_out[...] = jnp.sum(table_in[...], axis=0)
    own.wait()
    own_small.wait()
    for copy in third:
        copy.wait()


def reduce_all(big, small, table, collective_id):
    return pl.pallas_call(
        reduce_kernel,
        out_shape=(
            jax.ShapeDtypeStruct(big.shape, big.dtype),
            jax.ShapeDtypeStruct(small.shape, small.dtype),
            jax.ShapeDtypeStruct(table.shape, table.dtype),
        ),
        in_specs=[VMEM] * 3,
        out_specs=(ANY, ANY, VMEM),
        scratch_shapes=[
            pltpu.VMEM(big.shape, big.dtype),
            pltpu.VMEM(big.shape[1:], big.dtype),
            pltpu.VMEM((2,) + small.shape, small.dtype),
            pltpu.VMEM(small.shape, small.dtype),
            pltpu.VMEM(small.shape, small.dtype),
            pltpu.VMEM(small.shape[1:], small.dtype),
            pltpu.VMEM((OWNERS,) + table.shape, table.dtype),
            pltpu.SemaphoreType.DMA((2,)),
            pltpu.SemaphoreType.DMA((5, 16)),
            pltpu.SemaphoreType.DMA((5, 16)),
            pltpu.SemaphoreType.DMA((2,)),
            pltpu.SemaphoreType.DMA((2,)),
        ],
        compiler_params=pltpu.CompilerParams(
            collective_id=collective_id, has_side_effects=True, vmem_limit_bytes=VMEM_BYTES
        ),
        name="reduce_all",
    )(big, small, table)


def bucket_of(offsets):
    distance = jnp.abs(offsets)
    far_bucket = 8 + sum(
        ((distance >= threshold).astype(jnp.int32) for threshold in (12, 16, 23, 32, 46, 64, 91))
    )
    near_far = jnp.where(distance < 8, distance, far_bucket)
    return near_far + 16 * (offsets > 0).astype(jnp.int32)


def offset_buckets():
    offsets = jnp.arange(2 * LEN, dtype=jnp.int32) - (LEN - 1)
    return (bucket_of(offsets)[:, None] == jnp.arange(32, dtype=jnp.int32)[None, :]).astype(jnp.float32)


def spread_matrices(route_ids, slot_ids):
    row = jnp.arange(WAVES * OWNERS * PIECE, dtype=jnp.int32)
    half, expert = row % 16 // 8, row % 8 // 4
    slot_row = row // (OWNERS * PIECE) * 4 + row % 4
    row_key = (half * EXPERTS + row // PIECE % OWNERS * 2 + expert) * (MICRO * CAP) + slot_row
    micro = jnp.arange(MICRO, dtype=jnp.int32)[:, None]
    token_key = (route_ids * (MICRO * CAP) + micro * CAP + slot_ids).reshape(-1)
    column_key = jnp.concatenate([token_key, token_key + EXPERTS * MICRO * CAP])
    return (
        (row_key[:, None] == column_key[None, :]).astype(jnp.bfloat16),
        (column_key[:, None] == row_key[None, :]).astype(jnp.bfloat16),
    )


def per_device(
    stream, norm_gains, attn_qkv, attn_out, rel_bias, router, expert_in, expert_out, routes, slots
):
    buckets = offset_buckets()
    by_offset = lax.dot_general(
        rel_bias[0], buckets, (((0,), (1,)), ((), ())), precision=lax.Precision.HIGHEST
    )
    by_offset = jnp.concatenate([by_offset, jnp.zeros((5, 2 * LEN), jnp.float32)], axis=0)
    chosen = (routes[0].reshape(-1)[:, None] == jnp.arange(EXPERTS, dtype=jnp.int32)[None, :]).astype(jnp.float32)
    common = (norm_gains[0], attn_qkv[0], attn_out[0], by_offset, router[0])
    common += spread_matrices(routes[0], slots[0]) + (chosen,) + sorting() + (expert_in[0], expert_out[0])
    is_first = lax.axis_index("section") == 0
    own = stream[0]

    early = layer_forward(own, common, None, 0, 0)
    *saved, output, incoming = layer_forward(own, common, early, 1, 1)
    saved = (*saved, incoming)
    late = layer_backward(own, common, saved, None, 1, 2)
    grads = layer_backward(own, common, saved, late, 0, 3)
    inner_grad, outer_grad, router_grad, gain_two, attend_grad, offset_grad, gain_one, input_grad = grads

    big = attend_grad.astype(jnp.bfloat16).reshape(OWNERS, 48, D)
    small = jnp.concatenate([router_grad, gain_one[:1], gain_two[:1]], axis=0)
    small = jnp.pad(small.reshape(-1), (0, 32768 - 34 * D))
    table = jnp.dot(offset_grad[:3], buckets, precision=lax.Precision.HIGHEST)
    table = jnp.pad(table, ((0, 5), (0, 96)))
    big, small, table = reduce_all(big, small.reshape(OWNERS, 8, 256), table, 4)
    big = big.reshape(4, WIDTH, D).astype(jnp.float32)
    small = small.reshape(-1)[: 34 * D].reshape(34, D)
    end_rows = jnp.where(is_first, input_grad, output)
    return (
        end_rows[None],
        small[32:][None],
        jnp.swapaxes(big[:3], 1, 2)[None],
        big[3][None],
        table[:3, :32].T[None],
        small[:32].T[None],
        inner_grad[None],
        outer_grad[None],
    )


def solution(mesh):
    return jax.shard_map(
        per_device,
        mesh=mesh,
        in_specs=(
            P("section", None, ("expert", "shard"), None),
            P("section", None, None),
            P("section", None, None, "shard"),
            P("section", "shard", None),
            P("section", None, "shard"),
            P("section", None, None),
            P("section", "expert", None, "shard"),
            P("section", "expert", "shard", None),
            P("section", None, ("expert", "shard")),
            P("section", None, ("expert", "shard")),
        ),
        out_specs=(
            P("section", None, ("expert", "shard"), None),
            P("section", None, None),
            P("section", None, None, "shard"),
            P("section", "shard", None),
            P("section", None, "shard"),
            P("section", None, None),
            P("section", "expert", None, "shard"),
            P("section", "expert", "shard", None),
        ),
        check_vma=False,
    )
```

```python
import functools

import jax
import jax.numpy as jnp
import numpy as np
from jax import lax
from jax.experimental import pallas as pl
from jax.experimental.pallas import tpu as pltpu
from jax.sharding import PartitionSpec as P

HEAD_DIM = 64
HEADS_HERE = 3
LEN = 512
MICRO = 2
ROWS = 128
D = 768
HALF = 384
EXPERTS = 32
CAP = 6
OWNERS = 16
WAVES = 3
PIECE = 16
VMEM_BYTES = 60 * 1024 * 1024
MESH = pl.DeviceIdType.MESH
ANY = pl.BlockSpec(memory_space=pl.ANY)
VMEM = pl.BlockSpec(memory_space=pltpu.VMEM)


def remote_to(src, dst, send, recv, device):
    return pltpu.make_async_remote_copy(
        src_ref=src, dst_ref=dst, send_sem=send, recv_sem=recv, device_id=device, device_id_type=MESH
    )


def remote(src, dst, send, recv, axis, index):
    return remote_to(src, dst, send, recv, {axis: index})


def greet(partners):
    barrier = pltpu.get_barrier_semaphore()
    for device in partners:
        pl.semaphore_signal(barrier, inc=1, device_id=device, device_id_type=MESH)
    return lambda: pl.semaphore_wait(barrier, len(partners))


def shard_places():
    me = lax.axis_index("shard")
    y, core = lax.div(me, 2), lax.rem(me, 2)
    return me, 2 * y + (1 - core), 2 * (1 - y) + core, 2 * (1 - y) + (1 - core)


def expert_places():
    me = lax.axis_index("expert")
    return me, lax.div(me, 4), lax.rem(me, 4)


def owner_at(x, z, dx, dz):
    return lax.rem(x + dx, 4) * 4 + lax.rem(z + dz, 4)


def all_owners(x, z):
    return [{"expert": owner_at(x, z, dx, dz)} for dx in range(4) for dz in range(4) if dx or dz]


class Cross:
    def __init__(self, sems):
        self.send, self.recv = sems
        self.device = {"shard": shard_places()[2]}

    def to(self, n, half, source, goal):
        return remote_to(source, goal, self.send.at[half, n], self.recv.at[half, n], self.device)

    def start(self, n, sources, goals):
        for half in range(2):
            self.to(n, half, sources[half], goals[half]).start()

    def wait_recv(self, n, goals):
        for half in range(2):
            self.to(n, half, goals[half], goals[half]).wait_recv()

    def wait_send(self, n, sources):
        for half in range(2):
            self.to(n, half, sources[half], sources[half]).wait_send()


def copy_all(sources, goals, sems, first=0):
    copies = [
        pltpu.make_async_copy(source, goal, sems.at[first + n]) for n, (source, goal) in enumerate(zip(sources, goals))
    ]
    for copy in copies:
        copy.start()

    def done():
        for copy in copies:
            copy.wait()

    return done


def dot(a, b, dims=((1,), (0,))):
    return lax.dot_general(a, b, (dims, ((), ())), preferred_element_type=jnp.float32)


NT = ((1,), (1,))
TN = ((0,), (0,))
WIDTH = HEADS_HERE * HEAD_DIM


def rms_norm(values, gain):
    return values * lax.rsqrt(jnp.mean(values * values, axis=-1, keepdims=True) + 1e-06) * gain


def rms_norm_back(values, gain, grad):
    scale = lax.rsqrt(jnp.mean(values * values, axis=-1, keepdims=True) + 1e-06)
    unit = values * scale
    unit_grad = grad * gain
    value_grad = scale * (unit_grad - unit * jnp.mean(unit_grad * unit, axis=-1, keepdims=True))
    return value_grad, jnp.sum(grad * unit, axis=0, keepdims=True)


def fill_bias(by_offset, bias):
    for head in range(HEADS_HERE):
        spread = jnp.broadcast_to(by_offset[pl.ds(head, 1), :], (LEN, 2 * LEN))
        bias[head] = pltpu.roll(spread, LEN + 1, 1, stride=1, stride_axis=0)[:, :LEN]


def head_of(array, head):
    return array[:, head * HEAD_DIM : (head + 1) * HEAD_DIM]


def softmax_rows(queries, keys, bias):
    scores = dot(queries, keys, NT) * 0.125 + bias
    raised = jnp.exp(scores - jnp.max(scores, axis=1, keepdims=True))
    return raised / jnp.sum(raised, axis=1, keepdims=True)


def row_halves(block):
    return [block.at[pl.ds(half * ROWS // 2, ROWS // 2)] for half in range(2)]


class Gather:
    def __init__(self, rows, sems):
        self.rows, self.send, self.recv = rows, sems[0], sems[1]
        self.cross_link = Cross(sems[2:])
        self.me, self.core, self.cross, _ = shard_places()

    def piece(self, m, whose, kind):
        block = self.rows.at[m, whose]
        at = 2 * kind + m
        return remote(block, block, self.send.at[at], self.recv.at[at], "shard", self.core)

    def start(self, m):
        block = row_halves(self.rows.at[m, self.me])
        self.cross_link.start(m, block, block)
        self.near(m).start()

    def near(self, m):
        return self.piece(m, self.me, 0)

    def on(self, m):
        return self.piece(m, self.cross, 1)

    def hand_on(self, m):
        self.cross_link.wait_recv(m, row_halves(self.rows.at[m, self.cross]))
        self.on(m).start()

    def finish(self, m):
        self.near(m).wait_recv()
        self.on(m).wait_recv()

    def drain(self):
        for m in range(MICRO):
            self.cross_link.wait_send(m, row_halves(self.rows.at[m, self.me]))
            self.near(m).wait_send()
            self.on(m).wait_send()


class HeadSum:
    def __init__(self, part, buffers, sems):
        self.part, self.send, self.recv = part, sems[0], sems[1]
        self.cross_link = Cross(sems[2:])
        self.pair, self.mine, self.theirs, self.crossed = buffers
        self.me, self.core, self.cross, self.diag = shard_places()

    def first(self, m):
        return remote(self.part.at[m, self.diag], self.theirs.at[m], self.send.at[m], self.recv.at[m], "shard", self.core)

    def second(self, m):
        return remote(
            self.part.at[m, self.core], self.mine.at[m], self.send.at[2 + m], self.recv.at[2 + m], "shard", self.core
        )

    def start(self, m):
        self.first(m).start()
        self.second(m).start()

    def cross_over(self, m):
        self.first(m).wait_recv()
        self.pair[m] = (self.part[m, self.cross].astype(jnp.float32) + self.theirs[m].astype(jnp.float32)).astype(
            jnp.bfloat16
        )
        self.cross_link.start(m, row_halves(self.pair.at[m]), row_halves(self.crossed.at[m]))

    def total(self, m):
        self.second(m).wait_recv()
        self.cross_link.wait_recv(m, row_halves(self.crossed.at[m]))
        return (
            self.part[m, self.me].astype(jnp.float32)
            + self.mine[m].astype(jnp.float32)
            + self.crossed[m].astype(jnp.float32)
        )

    def drain(self):
        for m in range(MICRO):
            self.first(m).wait_send()
            self.second(m).wait_send()
            self.cross_link.wait_send(m, row_halves(self.pair.at[m]))


SHARD_BUFFERS = (
    [pltpu.VMEM((MICRO, 4, ROWS, D), jnp.bfloat16)]
    + [pltpu.VMEM((MICRO, ROWS, D), jnp.bfloat16)] * 4
)
SHARD_SEMS = ([pltpu.SemaphoreType.DMA((4,))] * 2 + [pltpu.SemaphoreType.DMA((2, MICRO))] * 2) * 2


def shard_group(gathered, buffers, sems):
    part = buffers[0]
    gather = Gather(gathered, sems[:4])
    heads_sum = HeadSum(part, buffers[1:], sems[4:])
    return gather, heads_sum, part


def attend(rows, qkv, wo, outs, bias, gather, heads_sum, part):
    normed_all, packed, mixed, middle = outs
    for m in range(MICRO):
        gather.hand_on(m)
    for m in range(MICRO):
        gather.finish(m)
        x = normed_all[m].reshape(LEN, D)
        q, k, v = [dot(x, qkv[which], NT).astype(jnp.bfloat16) for which in range(3)]
        packed[m, 0] = q
        packed[m, 1] = k
        packed[m, 2] = v
        if m:
            heads_sum.cross_over(m - 1)
        heads = []
        for head in range(HEADS_HERE):
            chances = softmax_rows(head_of(q, head), head_of(k, head), bias[head]).astype(jnp.bfloat16)
            heads.append(dot(chances, head_of(v, head)).astype(jnp.bfloat16))
        together = jnp.concatenate(heads, axis=1)
        mixed[m] = together
        part[m] = dot(together, wo[...]).astype(jnp.bfloat16).reshape(4, ROWS, D)
        heads_sum.start(m)
    heads_sum.cross_over(MICRO - 1)
    for m in range(MICRO):
        middle[m] = rows[m].astype(jnp.float32) + heads_sum.total(m)


def attend_back(
    middle_grad, rows, gains, normed_all, packed, mixed, qkv, wo, outs, grad_all, bias, gather, heads_sum, part, beside, done
):
    input_grad, weight_grad, offset_grad, gain_grad = outs
    me = shard_places()[0]
    for m in range(MICRO):
        grad_all[m, me] = middle_grad[m].astype(jnp.bfloat16)
        gather.start(m)
    beside(0)
    offset_grad[...] = jnp.zeros_like(offset_grad)
    row = lax.broadcasted_iota(jnp.int32, (LEN, LEN), 0)
    column = lax.broadcasted_iota(jnp.int32, (LEN, LEN), 1)
    backwards = (row + column == LEN - 1).astype(jnp.bfloat16)
    for m in range(MICRO):
        gather.hand_on(m)
    beside(1)
    for m in range(MICRO):
        gather.finish(m)
        grad = grad_all[m].reshape(LEN, D)
        mixed_grad = dot(grad, wo[...], NT).astype(jnp.bfloat16)
        if m:
            heads_sum.cross_over(m - 1)
        q, k, v = packed[m, 0], packed[m, 1], packed[m, 2]
        q_grads, k_grads, v_grads = [], [], []
        for head in range(HEADS_HERE):
            q_head, k_head, v_head = head_of(q, head), head_of(k, head), head_of(v, head)
            grad_head = head_of(mixed_grad, head)
            chances = softmax_rows(q_head, k_head, bias[head])
            grad_chances = dot(grad_head, v_head, NT)
            weighed = jnp.sum(chances * grad_chances, axis=1, keepdims=True)
            grad_scores = (chances * (grad_chances - weighed)).astype(jnp.bfloat16)
            q_grads.append((dot(grad_scores, k_head) * 0.125).astype(jnp.bfloat16))
            k_grads.append((dot(grad_scores, q_head, TN) * 0.125).astype(jnp.bfloat16))
            v_grads.append(dot(chances.astype(jnp.bfloat16), grad_head, TN).astype(jnp.bfloat16))
            turned = dot(backwards, grad_scores)
            wide = jnp.concatenate([turned, jnp.zeros_like(turned)], axis=1)
            aligned = pltpu.roll(wide, 0, 1, stride=1, stride_axis=0)
            offset_grad[pl.ds(head, 1), :] += jnp.sum(aligned, axis=0, keepdims=True)
        grads = [jnp.concatenate(pieces, axis=1) for pieces in (q_grads, k_grads, v_grads)]
        summed = dot(grads[0], qkv[0]) + dot(grads[1], qkv[1]) + dot(grads[2], qkv[2])
        part[m] = summed.astype(jnp.bfloat16).reshape(4, ROWS, D)
        heads_sum.start(m)
        if m:
            heads_sum.cross_over(m)
        x = normed_all[m].reshape(LEN, D)
        for which in range(4):
            left = grads[which] if which < 3 else mixed[m]
            added = dot(left, x if which < 3 else grad, TN)
            where = pl.ds(which * WIDTH, WIDTH)
            weight_grad[where, :] = added if m == 0 else weight_grad[where, :] + added
        beside(2 + m)
    gain_total = jnp.zeros((1, D), jnp.float32)
    for m in range(MICRO):
        back, gain_part = rms_norm_back(rows[m].astype(jnp.float32), gains[0:1, :], heads_sum.total(m))
        input_grad[m] = (middle_grad[m] + back).astype(jnp.bfloat16)
        done(m)
        gain_total = gain_total + gain_part
    gain_grad[...] = gain_total


GROUP_ROWS = 16 * PIECE
SORTED = 16 * 4
WAVE_ROWS = 4 * SORTED
PAIRS = [(dx, dz) for dx in range(4) for dz in range(4) if dx or dz]


def sorting():
    order = np.zeros((GROUP_ROWS, GROUP_ROWS), np.float32)
    for e in range(2):
        for half in range(2):
            for sender in range(16):
                for at in range(4):
                    order[(e * 2 + half) * SORTED + sender * 4 + at, sender * PIECE + half * 8 + e * 4 + at] = 1
    return jnp.asarray(order, jnp.bfloat16), jnp.asarray(order.T, jnp.bfloat16)


def sender_halves(block):
    return [block.at[pl.ds(8 * half, 8)] for half in range(2)]


class SlotsOut:
    def __init__(self, slots, arrived, sems):
        self.slots, self.arrived = slots, arrived
        self.send_x, self.recv_x, self.send_y, self.recv_y = sems[:4]
        self.cross_link = Cross(sems[4:])
        self.me, self.core, self.cross, _ = shard_places()
        self.here, self.px, self.pz = expert_places()

    def away(self, w, dx, dz):
        at = w * 16 + dx * 4 + dz
        goal = owner_at(self.px, self.pz, dx, dz)
        return remote(
            self.slots.at[w, goal],
            self.arrived.at[self.me, w, self.here],
            self.send_x.at[at],
            self.recv_x.at[at],
            "expert",
            goal,
        )

    def piece(self, w, whose, kind):
        block = self.arrived.at[whose, w]
        at = WAVES * kind + w
        return remote(block, block, self.send_y.at[at], self.recv_y.at[at], "shard", self.core)

    def near(self, w):
        return self.piece(w, self.me, 0)

    def on(self, w):
        return self.piece(w, self.cross, 1)

    def start(self, w):
        for dx, dz in PAIRS:
            self.away(w, dx, dz).start()
        self.arrived[self.me, w, self.here] = self.slots[w, self.here]

    def sent(self, w):
        for dx, dz in PAIRS:
            self.away(w, dx, dz).wait_send()

    def spread_on(self, w):
        for dx, dz in PAIRS:
            self.away(w, dx, dz).wait_recv()
        block = sender_halves(self.arrived.at[self.me, w])
        self.cross_link.start(w, block, block)
        self.near(w).start()

    def hand_on(self, w):
        self.cross_link.wait_recv(w, sender_halves(self.arrived.at[self.cross, w]))
        self.on(w).start()

    def finish(self, w):
        self.near(w).wait_recv()
        self.on(w).wait_recv()

    def drain(self):
        for w in range(WAVES):
            self.cross_link.wait_send(w, sender_halves(self.arrived.at[self.me, w]))
            self.near(w).wait_send()
            self.on(w).wait_send()


class SlotsBack:
    def __init__(self, part, returned, buffers, sems):
        self.part, self.returned = part, returned
        self.pair, self.mine, self.theirs, self.crossed, self.total = buffers
        self.send_x, self.recv_x, self.send_y, self.recv_y = sems[:4]
        self.cross_link = Cross(sems[4:])
        self.me, self.core, self.cross, self.diag = shard_places()
        self.here, self.px, self.pz = expert_places()

    def to_core(self, w, whose, buffer, kind):
        at = WAVES * kind + w
        return remote(self.part.at[whose, w], buffer.at[w], self.send_y.at[at], self.recv_y.at[at], "shard", self.core)

    def first(self, w):
        return self.to_core(w, self.diag, self.theirs, 0)

    def second(self, w):
        return self.to_core(w, self.core, self.mine, 1)

    def away(self, w, dx, dz):
        at = w * 16 + dx * 4 + dz
        goal = owner_at(self.px, self.pz, dx, dz)
        return remote(
            self.total.at[w, goal],
            self.returned.at[w, self.here],
            self.send_x.at[at],
            self.recv_x.at[at],
            "expert",
            goal,
        )

    def start(self, w):
        self.first(w).start()
        self.second(w).start()

    def cross_over(self, w):
        self.first(w).wait_recv()
        self.pair[w] = (self.part[self.cross, w].astype(jnp.float32) + self.theirs[w].astype(jnp.float32)).astype(
            jnp.bfloat16
        )
        self.cross_link.start(w, sender_halves(self.pair.at[w]), sender_halves(self.crossed.at[w]))

    def send_home(self, w):
        self.second(w).wait_recv()
        self.cross_link.wait_recv(w, sender_halves(self.crossed.at[w]))
        self.total[w] = (
            self.part[self.me, w].astype(jnp.float32)
            + self.mine[w].astype(jnp.float32)
            + self.crossed[w].astype(jnp.float32)
        ).astype(jnp.bfloat16)
        for dx, dz in PAIRS:
            self.away(w, dx, dz).start()
        self.returned[w, self.here] = self.total[w, self.here]

    def finish(self):
        for w in range(WAVES):
            for dx, dz in PAIRS:
                self.away(w, dx, dz).wait_recv()

    def drain(self):
        for w in range(WAVES):
            self.first(w).wait_send()
            self.second(w).wait_send()
            self.cross_link.wait_send(w, sender_halves(self.pair.at[w]))
            for dx, dz in PAIRS:
                self.away(w, dx, dz).wait_send()


def one_hot(equal):
    return jnp.where(equal, 1.0, 0.0).astype(jnp.bfloat16)


def to_slots(token_row, slot_column, rows, slots):
    stacked = jnp.concatenate([rows[:, :HALF], rows[:, HALF:]], axis=0)
    spread = one_hot(slot_column[...] == token_row[...])
    slots[...] = dot(spread, stacked).astype(jnp.bfloat16).reshape(WAVES, OWNERS, PIECE, HALF)


def from_slots(token_column, slot_row, slots):
    spread_t = one_hot(token_column[...] == slot_row[...])
    stacked = dot(spread_t, slots[...].reshape(WAVES * OWNERS * PIECE, HALF))
    return jnp.concatenate([stacked[: MICRO * ROWS], stacked[MICRO * ROWS :]], axis=1)


def chosen_experts(route_column):
    experts_here = lax.broadcasted_iota(jnp.int32, (MICRO * ROWS, EXPERTS), 1)
    return jnp.where(route_column[...] == experts_here, 1.0, 0.0)


def sort_in(order, arrived, w, rows, base):
    for group in range(4):
        picked = dot(order, arrived[group, w].reshape(GROUP_ROWS, HALF)).astype(jnp.bfloat16)
        for e in range(2):
            for half in range(2):
                at = (2 * e + half) * SORTED
                rows[e, pl.ds(base + group * SORTED, SORTED), half * HALF : (half + 1) * HALF] = picked[at : at + SORTED]


def sort_out(order_t, results, part, w):
    for group in range(4):
        where = slice(group * SORTED, (group + 1) * SORTED)
        pieces = [results[e, where, half * HALF : (half + 1) * HALF] for e in range(2) for half in range(2)]
        block = dot(order_t, jnp.concatenate(pieces, axis=0)).astype(jnp.bfloat16)
        part[group, w] = block.reshape(OWNERS, PIECE, HALF)


SCALE = 0.7978845608028654
CUBIC = 0.044715


def flat(rows):
    return rows.reshape(MICRO * ROWS, D)


SLOT_SEMS = (
    [pltpu.SemaphoreType.DMA((16 * WAVES,))] * 2
    + [pltpu.SemaphoreType.DMA((2 * WAVES,))] * 2
    + [pltpu.SemaphoreType.DMA((2, WAVES))] * 2
) * 2
SLOT_BUFFERS = (
    [pltpu.VMEM((WAVES, OWNERS, PIECE, HALF), jnp.bfloat16)] * 2
    + [pltpu.VMEM((4, WAVES, OWNERS, PIECE, HALF), jnp.bfloat16)]
    + [pltpu.VMEM((WAVES, OWNERS, PIECE, HALF), jnp.bfloat16)] * 5
)


def slot_exchange(arrived, buffers, sems):
    slots, returned, part, *sums = buffers
    out = SlotsOut(slots, arrived, sems[:6])
    back = SlotsBack(part, returned, sums, sems[6:])
    return out, back


def pipeline(out, back, beside, compute):
    out.start(0)
    beside()
    out.sent(0)
    out.start(1)
    out.spread_on(0)
    out.sent(1)
    out.start(2)
    out.spread_on(1)
    out.hand_on(0)
    out.sent(2)
    out.spread_on(2)
    out.hand_on(1)
    out.finish(0)
    compute(0)
    back.start(0)
    out.hand_on(2)
    out.finish(1)
    back.cross_over(0)
    compute(1)
    back.start(1)
    out.finish(2)
    back.cross_over(1)
    back.send_home(0)
    compute(2)
    out.drain()
    back.start(2)
    back.send_home(1)
    back.cross_over(2)


def experts(middle, gains, router, keys, order, order_t, inner, outer, fetched, outs, arrived, results, out, back):
    rows, normed_two, router_prob, gating, expert_rows, output = outs
    token_row, token_column, slot_row, slot_column, route_column = keys
    normed = rms_norm(flat(middle[...]), gains[1:2, :]).astype(jnp.bfloat16)
    normed_two[...] = normed
    to_slots(token_row, slot_column, normed, out.slots)

    def beside():
        logits = dot(normed, router[...], NT)
        raised = jnp.exp(logits - jnp.max(logits, axis=1, keepdims=True))
        prob = raised / jnp.sum(raised, axis=1, keepdims=True)
        router_prob[...] = prob
        gating[...] = jnp.sum(prob * chosen_experts(route_column), axis=1, keepdims=True)
        fetched()

    def compute(w):
        sort_in(order[...], arrived, w, rows, w * WAVE_ROWS)

        def one_expert(e, _):
            pre = dot(rows[e, pl.ds(w * WAVE_ROWS, WAVE_ROWS), :], inner[e])
            hidden = 0.5 * pre * (1 + jnp.tanh(SCALE * (pre + CUBIC * pre * pre * pre)))
            results[e] = dot(hidden.astype(jnp.bfloat16), outer[e]).astype(jnp.bfloat16)
            return 0

        lax.fori_loop(0, 2, one_expert, 0)
        sort_out(order_t[...], results, back.part, w)

    pipeline(out, back, beside, compute)
    back.send_home(WAVES - 1)
    back.finish()
    found = from_slots(token_column, slot_row, back.returned)
    expert_rows[...] = found.astype(jnp.bfloat16)
    output[...] = (flat(middle[...]) + gating[...] * found).astype(jnp.bfloat16).reshape(MICRO, ROWS, D)


def experts_back(
    grad_out,
    middle,
    normed_two,
    router_prob,
    gating,
    expert_rows,
    gains,
    router,
    keys,
    order,
    order_t,
    inner,
    outer,
    outs,
    middle_grad,
    grad_arrived,
    scratch,
    local,
    out,
    back,
):
    inner_grad, outer_grad, router_grad, gain_grad = outs
    rows, grads, hiddens, pre_grads, results = scratch
    token_row, token_column, slot_row, slot_column, route_column = keys
    grad = flat(grad_out[...]).astype(jnp.float32)
    to_slots(token_row, slot_column, (gating[...] * grad).astype(jnp.bfloat16), out.slots)
    gate_grad = jnp.sum(grad * expert_rows[...].astype(jnp.float32), axis=1, keepdims=True)
    logit_grad = ((gate_grad * gating[...]) * (chosen_experts(route_column) - router_prob[...])).astype(jnp.bfloat16)

    def beside():
        router_grad[...] = dot(logit_grad, normed_two[...], TN)

    def compute(w):
        base = w * WAVE_ROWS
        where = pl.ds(base, WAVE_ROWS)
        sort_in(order[...], grad_arrived, w, grads, base)

        def one_expert(e, _):
            pre = dot(rows[e, where, :], inner[e])
            squared = pre * pre
            bent = jnp.tanh(SCALE * pre * (1 + CUBIC * squared))
            slope = 0.5 * (1 + bent) + 0.5 * pre * (1 - bent * bent) * SCALE * (1 + 3 * CUBIC * squared)
            hiddens[e, where, :] = (0.5 * pre * (1 + bent)).astype(jnp.bfloat16)
            pre_grad = (dot(grads[e, where, :], outer[e], NT) * slope).astype(jnp.bfloat16)
            pre_grads[e, where, :] = pre_grad
            results[e] = dot(pre_grad, inner[e], NT).astype(jnp.bfloat16)
            return 0

        lax.fori_loop(0, 2, one_expert, 0)
        sort_out(order_t[...], results, back.part, w)

    writes = []

    def weight_grads(number, left, right, held, goal):
        def one_expert(e, _):
            for at in range(0, D, 256):
                held[e, at : at + 256, :] = dot(left[e, :, at : at + 256], right[e], TN).astype(jnp.bfloat16)
            return 0

        lax.fori_loop(0, 2, one_expert, 0)
        write = pltpu.make_async_copy(held, goal, local.at[number])
        write.start()
        writes.append(write)

    pipeline(out, back, beside, compute)
    weight_grads(0, rows, pre_grads, inner, inner_grad)
    back.send_home(WAVES - 1)
    weight_grads(1, hiddens, grads, outer, outer_grad)
    back.finish()
    normed_grad = dot(logit_grad, router[...]) + from_slots(token_column, slot_row, back.returned)
    value_grad, gain_part = rms_norm_back(flat(middle[...]), gains[1:2, :], normed_grad)
    middle_grad[...] = (grad + value_grad).reshape(MICRO, ROWS, D)
    gain_grad[...] = gain_part
    return writes


def over_section(source, goal, sems, m):
    other = 1 - lax.axis_index("section")
    return remote(source.at[m], goal.at[m], sems.at[0, m], sems.at[1, m], "section", other)


def greet_all():
    _, px, pz = expert_places()
    _, core, cross, _ = shard_places()
    peer = {"section": 1 - lax.axis_index("section")}
    return greet([{"shard": core}, {"shard": cross}, peer] + all_owners(px, pz))


SECTION_SEM = pltpu.SemaphoreType.DMA((2, MICRO))
LOCAL_SEM = pltpu.SemaphoreType.DMA((4,))
ROW_BLOCK = (MICRO, ROWS, D)


class Sums:
    def __init__(self, sources, outs, buffers, sems):
        self.big, self.small, self.table, self.gain = sources
        self.big_out, self.small_out, self.table_out, self.gain_out = outs
        self.big_in, self.big_sum, self.pair, self.small_in, self.small_sum = buffers[:5]
        self.table_in, self.gain_pair, self.gain_in = buffers[5:]
        self.sends, self.recvs, self.pair_send, self.pair_recv = sems
        self.me, self.core, self.cross, _ = shard_places()
        self.here, self.px, self.pz = expert_places()

    def each(self, kind, source, goal):
        copies = []
        for dx, dz in PAIRS:
            at, owner = dx * 4 + dz, owner_at(self.px, self.pz, dx, dz)
            copies.append(
                remote(source(owner), goal, self.sends.at[kind, at], self.recvs.at[kind, at], "expert", owner)
            )
            copies[-1].start()
        return copies

    def swap(self, n, source, goal, device):
        copy = remote(source, goal, self.pair_send.at[n], self.pair_recv.at[n], "shard", device)
        copy.start()
        return copy

    def small_near(self):
        self.near = self.swap(0, self.small, self.pair.at[0], self.core)

    def small_far(self):
        self.near.wait()
        self.small[...] += self.pair[0]
        self.far = self.swap(1, self.small, self.pair.at[1], self.cross)

    def small_away(self):
        self.far.wait()
        self.small[...] += self.pair[1]
        self.second = self.each(3, lambda owner: self.small.at[owner], self.small_in.at[self.here])
        self.small_in[self.here] = self.small[self.here]

    def small_home(self):
        for copy in self.second:
            copy.wait()
        self.small_sum[...] = jnp.sum(self.small_in[...], axis=0)
        self.third = self.each(4, lambda owner: self.small_sum, self.small_out.at[self.here])
        self.small_out[self.here] = self.small_sum[...]

    def big_away(self):
        self.first = self.each(0, lambda owner: self.big.at[owner], self.big_in.at[self.here])
        self.tables = self.each(1, lambda owner: self.table, self.table_in.at[self.here])
        self.big_in[self.here] = self.big[self.here]
        self.table_in[self.here] = self.table[...]

    def finish(self):
        near = self.swap(2, self.gain, self.gain_pair.at[0], self.core)
        near.wait()
        self.gain[...] += self.gain_pair[0]
        far = self.swap(3, self.gain, self.gain_pair.at[1], self.cross)
        far.wait()
        self.gain[...] += self.gain_pair[1]
        gains = self.each(5, lambda owner: self.gain, self.gain_in.at[self.here])
        self.gain_in[self.here] = self.gain[...]
        for copy in self.first:
            copy.wait()
        self.big_sum[...] = jnp.sum(self.big_in[...].astype(jnp.float32), axis=0).astype(jnp.bfloat16)
        last = self.each(2, lambda owner: self.big_sum, self.big_out.at[self.here])
        self.big_out[self.here] = self.big_sum[...]
        for copy in self.tables:
            copy.wait()
        self.table_out[...] = jnp.sum(self.table_in[...], axis=0)
        for copy in gains:
            copy.wait()
        self.gain_out[...] = jnp.sum(self.gain_in[...], axis=0)
        for copy in self.third + last:
            copy.wait()


BIG = (OWNERS, 4 * WIDTH // OWNERS, D)
SMALL = (OWNERS, 8, 256)
TABLE = (8, 128)
SUM_SCRATCH = [
    pltpu.VMEM(BIG, jnp.bfloat16),
    pltpu.VMEM(BIG[1:], jnp.bfloat16),
    pltpu.VMEM((2,) + SMALL, jnp.float32),
    pltpu.VMEM(SMALL, jnp.float32),
    pltpu.VMEM(SMALL[1:], jnp.float32),
    pltpu.VMEM((OWNERS,) + TABLE, jnp.float32),
    pltpu.VMEM((2,) + TABLE, jnp.float32),
    pltpu.VMEM((OWNERS,) + TABLE, jnp.float32),
]
SUM_SEMS = [pltpu.SemaphoreType.DMA((6, 16))] * 2 + [pltpu.SemaphoreType.DMA((4,))] * 2
OUTS = (
    jax.ShapeDtypeStruct(ROW_BLOCK, jnp.bfloat16),
    jax.ShapeDtypeStruct(BIG, jnp.bfloat16),
    jax.ShapeDtypeStruct(SMALL, jnp.float32),
    jax.ShapeDtypeStruct(TABLE, jnp.float32),
    jax.ShapeDtypeStruct(TABLE, jnp.float32),
    jax.ShapeDtypeStruct((2, D, D), jnp.bfloat16),
    jax.ShapeDtypeStruct((2, D, D), jnp.bfloat16),
)
STATE = [
    pltpu.VMEM((MICRO, 4, ROWS, D), jnp.bfloat16),
    pltpu.VMEM((MICRO, 3, LEN, WIDTH), jnp.bfloat16),
    pltpu.VMEM((MICRO, LEN, WIDTH), jnp.bfloat16),
    pltpu.VMEM(ROW_BLOCK, jnp.float32),
    pltpu.VMEM((2, WAVES * WAVE_ROWS, D), jnp.bfloat16),
    pltpu.VMEM((MICRO * ROWS, D), jnp.bfloat16),
    pltpu.VMEM((MICRO * ROWS, EXPERTS), jnp.float32),
    pltpu.VMEM((MICRO * ROWS, 1), jnp.float32),
    pltpu.VMEM((MICRO * ROWS, D), jnp.bfloat16),
    pltpu.VMEM(ROW_BLOCK, jnp.bfloat16),
]
GRADS = [
    pltpu.VMEM(ROW_BLOCK, jnp.bfloat16),
    pltpu.VMEM(ROW_BLOCK, jnp.float32),
    pltpu.VMEM(ROW_BLOCK, jnp.bfloat16),
    pltpu.VMEM((MICRO, 4, ROWS, D), jnp.bfloat16),
    pltpu.VMEM((4 * WIDTH, D), jnp.float32),
    pltpu.VMEM((8, 2 * LEN), jnp.float32),
    pltpu.VMEM((EXPERTS, D), jnp.float32),
    pltpu.VMEM((1, D), jnp.float32),
    pltpu.VMEM((1, D), jnp.float32),
    pltpu.VMEM(BIG, jnp.bfloat16),
    pltpu.VMEM(SMALL, jnp.float32),
    pltpu.VMEM(TABLE, jnp.float32),
    pltpu.VMEM(TABLE, jnp.float32),
]
WORK = (
    [
        pltpu.VMEM(ROW_BLOCK, jnp.bfloat16),
        pltpu.VMEM((HEADS_HERE, LEN, LEN), jnp.float32),
        pltpu.VMEM((2, D, D), jnp.bfloat16),
        pltpu.VMEM((2, D, D), jnp.bfloat16),
        pltpu.VMEM((4, WAVES, OWNERS, PIECE, HALF), jnp.bfloat16),
        SECTION_SEM,
        SECTION_SEM,
        LOCAL_SEM,
    ]
    + [pltpu.VMEM((2, WAVES * WAVE_ROWS, D), jnp.bfloat16)] * 3
    + [pltpu.VMEM((2, WAVE_ROWS, D), jnp.bfloat16)]
)
INPUTS = 14


def layers_kernel(
    own,
    gains,
    qkv,
    wo,
    by_offset,
    router,
    token_row,
    token_column,
    slot_row,
    slot_column,
    route_column,
    order,
    order_t,
    buckets,
    inner,
    outer,
    *refs,
):
    outs, refs = refs[:7], refs[7:]
    state, refs = refs[:10], refs[10:]
    grads, refs = refs[:13], refs[13:]
    incoming, bias, inner_here, outer_here, arrived, section, section_back, local = refs[:8]
    wide, refs = refs[8:12], refs[12:]
    shard_buffers, slot_buffers, refs = refs[:5], refs[5:13], refs[13:]
    shard_sems, slot_sems, refs = refs[:8], refs[8:20], refs[20:]
    normed_all, packed, mixed, middle, rows, normed_two, router_prob, gating, expert_rows, output = state
    grad_out, middle_grad, input_grad, grad_all, weight_grad, offset_grad, router_grad, gain_one, gain_two = grads[:9]
    sources = grads[9:]
    grads_wide, hiddens, pre_grads, results = wide
    gather, heads_sum, part = shard_group(normed_all, shard_buffers, shard_sems)
    gather_back, heads_sum_back, _ = shard_group(grad_all, shard_buffers, shard_sems)
    out, back = slot_exchange(arrived, slot_buffers, slot_sems)
    sums = Sums(sources, outs[1:5], refs[:8], refs[8:])
    keys = (token_row, token_column, slot_row, slot_column, route_column)
    first = lax.axis_index("section") == 0
    second = jnp.logical_not(first)
    me = shard_places()[0]

    ready = greet_all()
    fetched = copy_all((inner, outer), (inner_here, outer_here), local, 2)
    fill_bias(by_offset, bias)
    ready()

    for m in range(MICRO):

        @pl.when(first)
        def _(m=m):
            incoming[m] = own[m]

        @pl.when(second)
        def _(m=m):
            over_section(output, incoming, section, m).wait_recv()

        normed_all[m, me] = rms_norm(incoming[m].astype(jnp.float32), gains[0:1, :]).astype(jnp.bfloat16)
        gather.start(m)
    attend(incoming, qkv, wo, state[:4], bias, gather, heads_sum, part)
    experts(
        middle, gains, router, keys, order, order_t, inner_here, outer_here, fetched, state[4:], arrived, results, out, back
    )
    for stage in (gather, heads_sum, back):
        stage.drain()

    for m in range(MICRO):

        @pl.when(first)
        def _(m=m):
            over_section(output, incoming, section, m).start()

        @pl.when(second)
        def _(m=m):
            outs[0][m] = output[m]
            grad_out[m] = own[m]

    @pl.when(first)
    def _():
        for m in range(MICRO):
            over_section(input_grad, grad_out, section_back, m).wait_recv()

    writes = experts_back(
        grad_out,
        middle,
        normed_two,
        router_prob,
        gating,
        expert_rows,
        gains,
        router,
        keys,
        order,
        order_t,
        inner_here,
        outer_here,
        (outs[5], outs[6], router_grad, gain_two),
        middle_grad,
        arrived,
        (rows, grads_wide, hiddens, pre_grads, results),
        local,
        out,
        back,
    )

    def beside(step):
        if step == 0:
            small = sources[1]
            extra = jnp.concatenate([gain_two[...], jnp.zeros((7, D), jnp.float32)], axis=0)
            for group in range(5):
                block = router_grad[group * 8 : group * 8 + 8, :] if group < 4 else extra
                for third in range(3):
                    small[group * 3 + third] = block[:, third * 256 : (third + 1) * 256]
            small[15] = jnp.zeros(SMALL[1:], jnp.float32)
            sums.small_near()
        if step == 1:
            sums.small_far()
        if step == 2:
            sums.small_away()
        if step == 3:
            sources[0][...] = weight_grad[...].astype(jnp.bfloat16).reshape(BIG)
            sources[2][...] = lax.dot_general(
                offset_grad[...], buckets[...], (((1,), (0,)), ((), ())), precision=lax.Precision.HIGHEST
            )
            sums.small_home()
            sums.big_away()

    def done(m):
        @pl.when(first)
        def _():
            outs[0][m] = input_grad[m]

        @pl.when(second)
        def _():
            over_section(input_grad, grad_out, section_back, m).start()

    attend_back(
        middle_grad,
        incoming,
        gains,
        normed_all,
        packed,
        mixed,
        qkv,
        wo,
        (input_grad, weight_grad, offset_grad, gain_one),
        grad_all,
        bias,
        gather_back,
        heads_sum_back,
        part,
        beside,
        done,
    )
    pieces = [gain_one[:, at : at + 128] for at in range(0, D, 128)]
    sources[3][...] = jnp.concatenate(pieces + [jnp.zeros((2, 128), jnp.float32)], axis=0)
    sums.finish()
    for stage in (back, gather_back, heads_sum_back):
        stage.drain()
    for m in range(MICRO):

        @pl.when(first)
        def _(m=m):
            over_section(output, incoming, section, m).wait_send()

        @pl.when(second)
        def _(m=m):
            over_section(input_grad, grad_out, section_back, m).wait_send()

    for write in writes:
        write.wait()


def both_layers(*arrays):
    return pl.pallas_call(
        layers_kernel,
        out_shape=OUTS,
        in_specs=[VMEM] * INPUTS + [ANY] * 2,
        out_specs=(VMEM,) * 5 + (ANY,) * 2,
        scratch_shapes=STATE
        + GRADS
        + WORK
        + SHARD_BUFFERS
        + SLOT_BUFFERS
        + SHARD_SEMS
        + SLOT_SEMS
        + SUM_SCRATCH
        + SUM_SEMS,
        compiler_params=pltpu.CompilerParams(collective_id=0, has_side_effects=True, vmem_limit_bytes=VMEM_BYTES),
        name="both_layers",
    )(*arrays)


def bucket_of(offsets):
    distance = jnp.abs(offsets)
    far_bucket = 8 + sum(
        ((distance >= threshold).astype(jnp.int32) for threshold in (12, 16, 23, 32, 46, 64, 91))
    )
    near_far = jnp.where(distance < 8, distance, far_bucket)
    return near_far + 16 * (offsets > 0).astype(jnp.int32)


def offset_buckets():
    offsets = jnp.arange(2 * LEN, dtype=jnp.int32) - (LEN - 1)
    return (bucket_of(offsets)[:, None] == jnp.arange(32, dtype=jnp.int32)[None, :]).astype(jnp.float32)


def slot_keys():
    row = np.arange(WAVES * OWNERS * PIECE)
    half, expert = row % 16 // 8, row % 8 // 4
    slot_row = row // (OWNERS * PIECE) * 4 + row % 4
    return ((half * EXPERTS + row // PIECE % OWNERS * 2 + expert) * (MICRO * CAP) + slot_row).astype(np.int32)


def token_keys(route_ids, slot_ids):
    micro = jnp.arange(MICRO, dtype=jnp.int32)[:, None]
    key = (route_ids * (MICRO * CAP) + micro * CAP + slot_ids).reshape(-1)
    return jnp.concatenate([key, key + EXPERTS * MICRO * CAP])


def per_device(
    stream, norm_gains, attn_qkv, attn_out, rel_bias, router, expert_in, expert_out, routes, slots
):
    buckets = offset_buckets()
    by_offset = lax.dot_general(
        rel_bias[0], buckets, (((0,), (1,)), ((), ())), precision=lax.Precision.HIGHEST
    )
    by_offset = jnp.concatenate([by_offset, jnp.zeros((5, 2 * LEN), jnp.float32)], axis=0)
    tokens, slot_rows = token_keys(routes[0], slots[0]), jnp.asarray(slot_keys())
    common = (norm_gains[0], jnp.swapaxes(attn_qkv[0], 1, 2), attn_out[0], by_offset, router[0].T)
    common += (tokens[None, :], tokens[:, None], slot_rows[None, :], slot_rows[:, None], routes[0].reshape(-1, 1))
    common += sorting() + (jnp.pad(buckets, ((0, 0), (0, 96))), expert_in[0], expert_out[0])
    end_rows, big, small, table, gain_one, inner_grad, outer_grad = both_layers(stream[0], *common)

    big = big.reshape(4, WIDTH, D).astype(jnp.float32)
    small = jnp.swapaxes(small[:15].reshape(5, 3, 8, 256), 1, 2).reshape(40, D)
    return (
        end_rows[None],
        jnp.concatenate([gain_one[:6].reshape(1, D), small[32:33]], axis=0)[None],
        jnp.swapaxes(big[:3], 1, 2)[None],
        big[3][None],
        table[:3, :32].T[None],
        small[:32].T[None],
        inner_grad.astype(jnp.float32)[None],
        outer_grad.astype(jnp.float32)[None],
    )


def solution(mesh):
    return jax.shard_map(
        per_device,
        mesh=mesh,
        in_specs=(
            P("section", None, ("expert", "shard"), None),
            P("section", None, None),
            P("section", None, None, "shard"),
            P("section", "shard", None),
            P("section", None, "shard"),
            P("section", None, None),
            P("section", "expert", None, "shard"),
            P("section", "expert", "shard", None),
            P("section", None, ("expert", "shard")),
            P("section", None, ("expert", "shard")),
        ),
        out_specs=(
            P("section", None, ("expert", "shard"), None),
            P("section", None, None),
            P("section", None, None, "shard"),
            P("section", "shard", None),
            P("section", None, "shard"),
            P("section", None, None),
            P("section", "expert", None, "shard"),
            P("section", "expert", "shard", None),
        ),
        check_vma=False,
    )
```

```python
import functools

import jax
import jax.numpy as jnp
import numpy as np
from jax import lax
from jax.experimental import pallas as pl
from jax.experimental.pallas import tpu as pltpu
from jax.sharding import PartitionSpec as P

HEAD_DIM = 64
HEADS_HERE = 3
LEN = 512
MICRO = 2
ROWS = 128
D = 768
HALF = 384
EXPERTS = 32
CAP = 6
OWNERS = 16
WAVES = 3
PIECE = 16
VMEM_BYTES = 60 * 1024 * 1024
MESH = pl.DeviceIdType.MESH
ANY = pl.BlockSpec(memory_space=pl.ANY)
VMEM = pl.BlockSpec(memory_space=pltpu.VMEM)


def remote_to(src, dst, send, recv, device):
    return pltpu.make_async_remote_copy(
        src_ref=src, dst_ref=dst, send_sem=send, recv_sem=recv, device_id=device, device_id_type=MESH
    )


def remote(src, dst, send, recv, axis, index):
    return remote_to(src, dst, send, recv, {axis: index})


def greet(partners):
    barrier = pltpu.get_barrier_semaphore()
    for device in partners:
        pl.semaphore_signal(barrier, inc=1, device_id=device, device_id_type=MESH)
    return lambda: pl.semaphore_wait(barrier, len(partners))


def shard_places():
    me = lax.axis_index("shard")
    y, core = lax.div(me, 2), lax.rem(me, 2)
    return me, 2 * y + (1 - core), 2 * (1 - y) + core, 2 * (1 - y) + (1 - core)


def expert_places():
    me = lax.axis_index("expert")
    return me, lax.div(me, 4), lax.rem(me, 4)


def owner_at(x, z, dx, dz):
    return lax.rem(x + dx, 4) * 4 + lax.rem(z + dz, 4)


def all_owners(x, z):
    return [{"expert": owner_at(x, z, dx, dz)} for dx in range(4) for dz in range(4) if dx or dz]


class Cross:
    def __init__(self, sems):
        self.send, self.recv = sems
        self.device = {"shard": shard_places()[2]}

    def to(self, n, half, source, goal):
        return remote_to(source, goal, self.send.at[half, n], self.recv.at[half, n], self.device)

    def start(self, n, sources, goals):
        for half in range(2):
            self.to(n, half, sources[half], goals[half]).start()

    def wait_recv(self, n, goals):
        for half in range(2):
            self.to(n, half, goals[half], goals[half]).wait_recv()

    def wait_send(self, n, sources):
        for half in range(2):
            self.to(n, half, sources[half], sources[half]).wait_send()


def copy_all(sources, goals, sems, first=0):
    copies = [
        pltpu.make_async_copy(source, goal, sems.at[first + n]) for n, (source, goal) in enumerate(zip(sources, goals))
    ]
    for copy in copies:
        copy.start()

    def done():
        for copy in copies:
            copy.wait()

    return done


def dot(a, b, dims=((1,), (0,))):
    return lax.dot_general(a, b, (dims, ((), ())), preferred_element_type=jnp.float32)


NT = ((1,), (1,))
TN = ((0,), (0,))
WIDTH = HEADS_HERE * HEAD_DIM


def rms_norm(values, gain):
    return values * lax.rsqrt(jnp.mean(values * values, axis=-1, keepdims=True) + 1e-06) * gain


def rms_norm_back(values, gain, grad):
    scale = lax.rsqrt(jnp.mean(values * values, axis=-1, keepdims=True) + 1e-06)
    unit = values * scale
    unit_grad = grad * gain
    value_grad = scale * (unit_grad - unit * jnp.mean(unit_grad * unit, axis=-1, keepdims=True))
    return value_grad, jnp.sum(grad * unit, axis=0, keepdims=True)


def fill_bias(by_offset, bias):
    for head in range(HEADS_HERE):
        spread = jnp.broadcast_to(by_offset[pl.ds(head, 1), :], (LEN, 2 * LEN))
        bias[head] = pltpu.roll(spread, LEN + 1, 1, stride=1, stride_axis=0)[:, :LEN]


def head_of(array, head):
    return array[:, head * HEAD_DIM : (head + 1) * HEAD_DIM]


def softmax_rows(queries, keys, bias):
    scores = dot(queries, keys, NT) * 0.125 + bias
    raised = jnp.exp(scores - jnp.max(scores, axis=1, keepdims=True))
    return raised / jnp.sum(raised, axis=1, keepdims=True)


def row_halves(block):
    return [block.at[pl.ds(half * ROWS // 2, ROWS // 2)] for half in range(2)]


class Gather:
    def __init__(self, rows, sems):
        self.rows, self.send, self.recv = rows, sems[0], sems[1]
        self.cross_link = Cross(sems[2:])
        self.me, self.core, self.cross, _ = shard_places()

    def piece(self, m, whose, kind):
        block = self.rows.at[m, whose]
        at = 2 * kind + m
        return remote(block, block, self.send.at[at], self.recv.at[at], "shard", self.core)

    def start(self, m):
        block = row_halves(self.rows.at[m, self.me])
        self.cross_link.start(m, block, block)
        self.near(m).start()

    def near(self, m):
        return self.piece(m, self.me, 0)

    def on(self, m):
        return self.piece(m, self.cross, 1)

    def hand_on(self, m):
        self.cross_link.wait_recv(m, row_halves(self.rows.at[m, self.cross]))
        self.on(m).start()

    def finish(self, m):
        self.near(m).wait_recv()
        self.on(m).wait_recv()

    def drain(self):
        for m in range(MICRO):
            self.cross_link.wait_send(m, row_halves(self.rows.at[m, self.me]))
            self.near(m).wait_send()
            self.on(m).wait_send()


class HeadSum:
    def __init__(self, part, buffers, sems):
        self.part, self.send, self.recv = part, sems[0], sems[1]
        self.cross_link = Cross(sems[2:])
        self.pair, self.mine, self.theirs, self.crossed = buffers
        self.me, self.core, self.cross, self.diag = shard_places()

    def first(self, m):
        return remote(self.part.at[m, self.diag], self.theirs.at[m], self.send.at[m], self.recv.at[m], "shard", self.core)

    def second(self, m):
        return remote(
            self.part.at[m, self.core], self.mine.at[m], self.send.at[2 + m], self.recv.at[2 + m], "shard", self.core
        )

    def start(self, m):
        self.first(m).start()
        self.second(m).start()

    def cross_over(self, m):
        self.first(m).wait_recv()
        self.pair[m] = (self.part[m, self.cross].astype(jnp.float32) + self.theirs[m].astype(jnp.float32)).astype(
            jnp.bfloat16
        )
        self.cross_link.start(m, row_halves(self.pair.at[m]), row_halves(self.crossed.at[m]))

    def total(self, m):
        self.second(m).wait_recv()
        self.cross_link.wait_recv(m, row_halves(self.crossed.at[m]))
        return (
            self.part[m, self.me].astype(jnp.float32)
            + self.mine[m].astype(jnp.float32)
            + self.crossed[m].astype(jnp.float32)
        )

    def drain(self):
        for m in range(MICRO):
            self.first(m).wait_send()
            self.second(m).wait_send()
            self.cross_link.wait_send(m, row_halves(self.pair.at[m]))


SHARD_BUFFERS = (
    [pltpu.VMEM((MICRO, 4, ROWS, D), jnp.bfloat16)]
    + [pltpu.VMEM((MICRO, ROWS, D), jnp.bfloat16)] * 4
)
SHARD_SEMS = ([pltpu.SemaphoreType.DMA((4,))] * 2 + [pltpu.SemaphoreType.DMA((2, MICRO))] * 2) * 2


def shard_group(gathered, buffers, sems):
    part = buffers[0]
    gather = Gather(gathered, sems[:4])
    heads_sum = HeadSum(part, buffers[1:], sems[4:])
    return gather, heads_sum, part


def attend(rows, qkv, wo, outs, bias, gather, heads_sum, part):
    normed_all, packed, mixed, middle = outs
    for m in range(MICRO):
        gather.hand_on(m)
    for m in range(MICRO):
        gather.finish(m)
        x = normed_all[m].reshape(LEN, D)
        q, k, v = [dot(x, qkv[which], NT).astype(jnp.bfloat16) for which in range(3)]
        packed[m, 0] = q
        packed[m, 1] = k
        packed[m, 2] = v
        if m:
            heads_sum.cross_over(m - 1)
        heads = []
        for head in range(HEADS_HERE):
            chances = softmax_rows(head_of(q, head), head_of(k, head), bias[head]).astype(jnp.bfloat16)
            heads.append(dot(chances, head_of(v, head)).astype(jnp.bfloat16))
        together = jnp.concatenate(heads, axis=1)
        mixed[m] = together
        part[m] = dot(together, wo[...]).astype(jnp.bfloat16).reshape(4, ROWS, D)
        heads_sum.start(m)
    heads_sum.cross_over(MICRO - 1)
    for m in range(MICRO):
        middle[m] = rows[m].astype(jnp.float32) + heads_sum.total(m)


def attend_back(
    middle_grad, rows, gains, normed_all, packed, mixed, qkv, wo, outs, grad_all, dqkv, bias, gather, heads_sum, part, beside, done
):
    input_grad, weight_grad, offset_grad, gain_grad = outs
    me = shard_places()[0]
    for m in range(MICRO):
        grad_all[m, me] = middle_grad[m].astype(jnp.bfloat16)
        gather.start(m)
    beside(0)
    offset_grad[...] = jnp.zeros_like(offset_grad)
    row = lax.broadcasted_iota(jnp.int32, (LEN, LEN), 0)
    column = lax.broadcasted_iota(jnp.int32, (LEN, LEN), 1)
    backwards = (row + column == LEN - 1).astype(jnp.bfloat16)
    for m in range(MICRO):
        gather.hand_on(m)
    beside(1)
    for m in range(MICRO):
        gather.finish(m)
        grad = grad_all[m].reshape(LEN, D)
        mixed_grad = dot(grad, wo[...], NT).astype(jnp.bfloat16)
        if m:
            heads_sum.cross_over(m - 1)
        q, k, v = packed[m, 0], packed[m, 1], packed[m, 2]
        q_grads, k_grads, v_grads = [], [], []
        for head in range(HEADS_HERE):
            q_head, k_head, v_head = head_of(q, head), head_of(k, head), head_of(v, head)
            grad_head = head_of(mixed_grad, head)
            chances = softmax_rows(q_head, k_head, bias[head])
            grad_chances = dot(grad_head, v_head, NT)
            weighed = jnp.sum(chances * grad_chances, axis=1, keepdims=True)
            grad_scores = (chances * (grad_chances - weighed)).astype(jnp.bfloat16)
            q_grads.append((dot(grad_scores, k_head) * 0.125).astype(jnp.bfloat16))
            k_grads.append((dot(grad_scores, q_head, TN) * 0.125).astype(jnp.bfloat16))
            v_grads.append(dot(chances.astype(jnp.bfloat16), grad_head, TN).astype(jnp.bfloat16))
            turned = dot(backwards, grad_scores)
            wide = jnp.concatenate([turned, jnp.zeros_like(turned)], axis=1)
            aligned = pltpu.roll(wide, 0, 1, stride=1, stride_axis=0)
            offset_grad[pl.ds(head, 1), :] += jnp.sum(aligned, axis=0, keepdims=True)
        grads = [jnp.concatenate(pieces, axis=1) for pieces in (q_grads, k_grads, v_grads)]
        for which in range(3):
            dqkv[m, which] = grads[which]
        summed = dot(grads[0], qkv[0]) + dot(grads[1], qkv[1]) + dot(grads[2], qkv[2])
        part[m] = summed.astype(jnp.bfloat16).reshape(4, ROWS, D)
        heads_sum.start(m)
        if m:
            heads_sum.cross_over(m)
        if m == 0:
            beside(2)
    both = MICRO * LEN
    for which in range(4):
        left = (dqkv[:, which] if which < 3 else mixed[...]).reshape(both, WIDTH)
        right = (normed_all if which < 3 else grad_all)[...].reshape(both, D)
        owners = slice(which * 4, which * 4 + 4)
        weight_grad[owners] = dot(left, right, TN).astype(jnp.bfloat16).reshape(4, WIDTH // 4, D)
    beside(3)
    gain_total = jnp.zeros((1, D), jnp.float32)
    for m in range(MICRO):
        back, gain_part = rms_norm_back(rows[m].astype(jnp.float32), gains[0:1, :], heads_sum.total(m))
        input_grad[m] = (middle_grad[m] + back).astype(jnp.bfloat16)
        done(m)
        gain_total = gain_total + gain_part
    gain_grad[...] = gain_total


GROUP_ROWS = 16 * PIECE
SORTED = 16 * 4
WAVE_ROWS = 4 * SORTED
PAIRS = [(dx, dz) for dx in range(4) for dz in range(4) if dx or dz]


def sorting():
    order = np.zeros((GROUP_ROWS, GROUP_ROWS), np.float32)
    for e in range(2):
        for half in range(2):
            for sender in range(16):
                for at in range(4):
                    order[(e * 2 + half) * SORTED + sender * 4 + at, sender * PIECE + half * 8 + e * 4 + at] = 1
    return jnp.asarray(order, jnp.bfloat16), jnp.asarray(order.T, jnp.bfloat16)


def sender_halves(block):
    return [block.at[pl.ds(8 * half, 8)] for half in range(2)]


class SlotsOut:
    def __init__(self, slots, arrived, sems):
        self.slots, self.arrived = slots, arrived
        self.send_x, self.recv_x, self.send_y, self.recv_y = sems[:4]
        self.cross_link = Cross(sems[4:])
        self.me, self.core, self.cross, _ = shard_places()
        self.here, self.px, self.pz = expert_places()

    def away(self, w, dx, dz):
        at = w * 16 + dx * 4 + dz
        goal = owner_at(self.px, self.pz, dx, dz)
        return remote(
            self.slots.at[w, goal],
            self.arrived.at[self.me, w, self.here],
            self.send_x.at[at],
            self.recv_x.at[at],
            "expert",
            goal,
        )

    def piece(self, w, whose, kind):
        block = self.arrived.at[whose, w]
        at = WAVES * kind + w
        return remote(block, block, self.send_y.at[at], self.recv_y.at[at], "shard", self.core)

    def near(self, w):
        return self.piece(w, self.me, 0)

    def on(self, w):
        return self.piece(w, self.cross, 1)

    def start(self, w):
        for dx, dz in PAIRS:
            self.away(w, dx, dz).start()
        self.arrived[self.me, w, self.here] = self.slots[w, self.here]

    def sent(self, w):
        for dx, dz in PAIRS:
            self.away(w, dx, dz).wait_send()

    def spread_on(self, w):
        for dx, dz in PAIRS:
            self.away(w, dx, dz).wait_recv()
        block = sender_halves(self.arrived.at[self.me, w])
        self.cross_link.start(w, block, block)
        self.near(w).start()

    def hand_on(self, w):
        self.cross_link.wait_recv(w, sender_halves(self.arrived.at[self.cross, w]))
        self.on(w).start()

    def finish(self, w):
        self.near(w).wait_recv()
        self.on(w).wait_recv()

    def drain(self):
        for w in range(WAVES):
            self.cross_link.wait_send(w, sender_halves(self.arrived.at[self.me, w]))
            self.near(w).wait_send()
            self.on(w).wait_send()


class SlotsBack:
    def __init__(self, part, returned, buffers, sems):
        self.part, self.returned = part, returned
        self.pair, self.mine, self.theirs, self.crossed, self.total = buffers
        self.send_x, self.recv_x, self.send_y, self.recv_y = sems[:4]
        self.cross_link = Cross(sems[4:])
        self.me, self.core, self.cross, self.diag = shard_places()
        self.here, self.px, self.pz = expert_places()

    def to_core(self, w, whose, buffer, kind):
        at = WAVES * kind + w
        return remote(self.part.at[whose, w], buffer.at[w], self.send_y.at[at], self.recv_y.at[at], "shard", self.core)

    def first(self, w):
        return self.to_core(w, self.diag, self.theirs, 0)

    def second(self, w):
        return self.to_core(w, self.core, self.mine, 1)

    def away(self, w, dx, dz):
        at = w * 16 + dx * 4 + dz
        goal = owner_at(self.px, self.pz, dx, dz)
        return remote(
            self.total.at[w, goal],
            self.returned.at[w, self.here],
            self.send_x.at[at],
            self.recv_x.at[at],
            "expert",
            goal,
        )

    def start(self, w):
        self.first(w).start()
        self.second(w).start()

    def cross_over(self, w):
        self.first(w).wait_recv()
        self.pair[w] = (self.part[self.cross, w].astype(jnp.float32) + self.theirs[w].astype(jnp.float32)).astype(
            jnp.bfloat16
        )
        self.cross_link.start(w, sender_halves(self.pair.at[w]), sender_halves(self.crossed.at[w]))

    def send_home(self, w):
        self.second(w).wait_recv()
        self.cross_link.wait_recv(w, sender_halves(self.crossed.at[w]))
        self.total[w] = (
            self.part[self.me, w].astype(jnp.float32)
            + self.mine[w].astype(jnp.float32)
            + self.crossed[w].astype(jnp.float32)
        ).astype(jnp.bfloat16)
        for dx, dz in PAIRS:
            self.away(w, dx, dz).start()
        self.returned[w, self.here] = self.total[w, self.here]

    def finish(self):
        for w in range(WAVES):
            for dx, dz in PAIRS:
                self.away(w, dx, dz).wait_recv()

    def drain(self):
        for w in range(WAVES):
            self.first(w).wait_send()
            self.second(w).wait_send()
            self.cross_link.wait_send(w, sender_halves(self.pair.at[w]))
            for dx, dz in PAIRS:
                self.away(w, dx, dz).wait_send()


def one_hot(equal):
    return jnp.where(equal, 1.0, 0.0).astype(jnp.bfloat16)


def to_slots(token_row, slot_column, rows, slots):
    stacked = jnp.concatenate([rows[:, :HALF], rows[:, HALF:]], axis=0)
    spread = one_hot(slot_column[...] == token_row[...])
    slots[...] = dot(spread, stacked).astype(jnp.bfloat16).reshape(WAVES, OWNERS, PIECE, HALF)


def from_slots(token_column, slot_row, slots):
    spread_t = one_hot(token_column[...] == slot_row[...])
    stacked = dot(spread_t, slots[...].reshape(WAVES * OWNERS * PIECE, HALF))
    return jnp.concatenate([stacked[: MICRO * ROWS], stacked[MICRO * ROWS :]], axis=1)


def chosen_experts(token_column):
    key = token_column[: MICRO * ROWS, :]
    start = lax.broadcasted_iota(jnp.int32, (MICRO * ROWS, EXPERTS), 1) * (MICRO * CAP)
    return jnp.where(jnp.logical_and(key >= start, key < start + MICRO * CAP), 1.0, 0.0)


def sort_in(order, arrived, w, rows, base):
    for group in range(4):
        picked = dot(order, arrived[group, w].reshape(GROUP_ROWS, HALF)).astype(jnp.bfloat16)
        for e in range(2):
            for half in range(2):
                at = (2 * e + half) * SORTED
                rows[e, pl.ds(base + group * SORTED, SORTED), half * HALF : (half + 1) * HALF] = picked[at : at + SORTED]


def sort_out(order_t, results, part, w):
    for group in range(4):
        where = slice(group * SORTED, (group + 1) * SORTED)
        pieces = [results[e, where, half * HALF : (half + 1) * HALF] for e in range(2) for half in range(2)]
        block = dot(order_t, jnp.concatenate(pieces, axis=0)).astype(jnp.bfloat16)
        part[group, w] = block.reshape(OWNERS, PIECE, HALF)


SCALE = 0.7978845608028654
CUBIC = 0.044715


def flat(rows):
    return rows.reshape(MICRO * ROWS, D)


SLOT_SEMS = (
    [pltpu.SemaphoreType.DMA((16 * WAVES,))] * 2
    + [pltpu.SemaphoreType.DMA((2 * WAVES,))] * 2
    + [pltpu.SemaphoreType.DMA((2, WAVES))] * 2
) * 2
SLOT_BUFFERS = (
    [pltpu.VMEM((WAVES, OWNERS, PIECE, HALF), jnp.bfloat16)] * 2
    + [pltpu.VMEM((4, WAVES, OWNERS, PIECE, HALF), jnp.bfloat16)]
    + [pltpu.VMEM((WAVES, OWNERS, PIECE, HALF), jnp.bfloat16)] * 5
)


def slot_exchange(arrived, buffers, sems):
    slots, returned, part, *sums = buffers
    out = SlotsOut(slots, arrived, sems[:6])
    back = SlotsBack(part, returned, sums, sems[6:])
    return out, back


def pipeline(out, back, beside, compute):
    out.start(0)
    beside()
    out.sent(0)
    out.start(1)
    out.spread_on(0)
    out.sent(1)
    out.start(2)
    out.spread_on(1)
    out.hand_on(0)
    out.sent(2)
    out.spread_on(2)
    out.hand_on(1)
    out.finish(0)
    compute(0)
    back.start(0)
    out.hand_on(2)
    out.finish(1)
    back.cross_over(0)
    compute(1)
    back.start(1)
    out.finish(2)
    back.cross_over(1)
    back.send_home(0)
    compute(2)
    out.drain()
    back.start(2)
    back.send_home(1)
    back.cross_over(2)


def experts(middle, gains, router, keys, order, order_t, inner, outer, fetched, outs, arrived, results, out, back):
    rows, normed_two, router_prob, gating, expert_rows, output = outs
    token_row, token_column, slot_row, slot_column = keys
    normed = rms_norm(flat(middle[...]), gains[1:2, :]).astype(jnp.bfloat16)
    normed_two[...] = normed
    to_slots(token_row, slot_column, normed, out.slots)

    def beside():
        logits = dot(normed, router[...], NT)
        raised = jnp.exp(logits - jnp.max(logits, axis=1, keepdims=True))
        prob = raised / jnp.sum(raised, axis=1, keepdims=True)
        router_prob[...] = prob
        gating[...] = jnp.sum(prob * chosen_experts(token_column), axis=1, keepdims=True)
        fetched()

    def compute(w):
        sort_in(order[...], arrived, w, rows, w * WAVE_ROWS)

        def one_expert(e, _):
            pre = dot(rows[e, pl.ds(w * WAVE_ROWS, WAVE_ROWS), :], inner[e])
            hidden = 0.5 * pre * (1 + jnp.tanh(SCALE * (pre + CUBIC * pre * pre * pre)))
            results[e] = dot(hidden.astype(jnp.bfloat16), outer[e]).astype(jnp.bfloat16)
            return 0

        lax.fori_loop(0, 2, one_expert, 0)
        sort_out(order_t[...], results, back.part, w)

    pipeline(out, back, beside, compute)
    back.send_home(WAVES - 1)
    back.finish()
    found = from_slots(token_column, slot_row, back.returned)
    expert_rows[...] = found.astype(jnp.bfloat16)
    output[...] = (flat(middle[...]) + gating[...] * found).astype(jnp.bfloat16).reshape(MICRO, ROWS, D)


def experts_back(
    grad_out,
    middle,
    normed_two,
    router_prob,
    gating,
    expert_rows,
    gains,
    router,
    keys,
    order,
    order_t,
    inner,
    outer,
    outs,
    middle_grad,
    grad_arrived,
    scratch,
    local,
    out,
    back,
):
    inner_grad, outer_grad, router_grad, gain_grad = outs
    rows, grads, hiddens, pre_grads, results = scratch
    token_row, token_column, slot_row, slot_column = keys
    grad = flat(grad_out[...]).astype(jnp.float32)
    to_slots(token_row, slot_column, (gating[...] * grad).astype(jnp.bfloat16), out.slots)
    gate_grad = jnp.sum(grad * expert_rows[...].astype(jnp.float32), axis=1, keepdims=True)
    logit_grad = ((gate_grad * gating[...]) * (chosen_experts(token_column) - router_prob[...])).astype(jnp.bfloat16)

    def beside():
        router_grad[...] = dot(logit_grad, normed_two[...], TN)

    def compute(w):
        base = w * WAVE_ROWS
        where = pl.ds(base, WAVE_ROWS)
        sort_in(order[...], grad_arrived, w, grads, base)

        def one_expert(e, _):
            pre = dot(rows[e, where, :], inner[e])
            squared = pre * pre
            bent = jnp.tanh(SCALE * pre * (1 + CUBIC * squared))
            slope = 0.5 * (1 + bent) + 0.5 * pre * (1 - bent * bent) * SCALE * (1 + 3 * CUBIC * squared)
            hiddens[e, where, :] = (0.5 * pre * (1 + bent)).astype(jnp.bfloat16)
            pre_grad = (dot(grads[e, where, :], outer[e], NT) * slope).astype(jnp.bfloat16)
            pre_grads[e, where, :] = pre_grad
            results[e] = dot(pre_grad, inner[e], NT).astype(jnp.bfloat16)
            return 0

        lax.fori_loop(0, 2, one_expert, 0)
        sort_out(order_t[...], results, back.part, w)

    writes = []

    def weight_grads(number, left, right, held, goal):
        def one_expert(e, _):
            for at in range(0, D, 256):
                held[e, at : at + 256, :] = dot(left[e, :, at : at + 256], right[e], TN).astype(jnp.bfloat16)
            return 0

        lax.fori_loop(0, 2, one_expert, 0)
        write = pltpu.make_async_copy(held, goal, local.at[number])
        write.start()
        writes.append(write)

    pipeline(out, back, beside, compute)
    weight_grads(0, rows, pre_grads, inner, inner_grad)
    back.send_home(WAVES - 1)
    weight_grads(1, hiddens, grads, outer, outer_grad)
    back.finish()
    normed_grad = dot(logit_grad, router[...]) + from_slots(token_column, slot_row, back.returned)
    value_grad, gain_part = rms_norm_back(flat(middle[...]), gains[1:2, :], normed_grad)
    middle_grad[...] = (grad + value_grad).reshape(MICRO, ROWS, D)
    gain_grad[...] = gain_part
    return writes


def over_section(source, goal, sems, m):
    other = 1 - lax.axis_index("section")
    return remote(source.at[m], goal.at[m], sems.at[0, m], sems.at[1, m], "section", other)


def greet_all():
    _, px, pz = expert_places()
    _, core, cross, _ = shard_places()
    peer = {"section": 1 - lax.axis_index("section")}
    return greet([{"shard": core}, {"shard": cross}, peer] + all_owners(px, pz))


SECTION_SEM = pltpu.SemaphoreType.DMA((2, MICRO))
LOCAL_SEM = pltpu.SemaphoreType.DMA((4,))
ROW_BLOCK = (MICRO, ROWS, D)


class Sums:
    def __init__(self, sources, outs, buffers, sems):
        self.big, self.small, self.table, self.gain = sources
        self.big_out, self.small_out, self.table_out, self.gain_out = outs
        self.big_in, self.big_sum, self.pair, self.small_in, self.small_sum = buffers[:5]
        self.table_in, self.gain_pair, self.gain_in = buffers[5:]
        self.sends, self.recvs, self.pair_send, self.pair_recv = sems
        self.me, self.core, self.cross, _ = shard_places()
        self.here, self.px, self.pz = expert_places()

    def each(self, kind, source, goal):
        copies = []
        for dx, dz in PAIRS:
            at, owner = dx * 4 + dz, owner_at(self.px, self.pz, dx, dz)
            copies.append(
                remote(source(owner), goal, self.sends.at[kind, at], self.recvs.at[kind, at], "expert", owner)
            )
            copies[-1].start()
        return copies

    def swap(self, n, source, goal, device):
        copy = remote(source, goal, self.pair_send.at[n], self.pair_recv.at[n], "shard", device)
        copy.start()
        return copy

    def small_near(self):
        self.near = self.swap(0, self.small, self.pair.at[0], self.core)

    def small_far(self):
        self.near.wait()
        self.small[...] += self.pair[0]
        self.far = self.swap(1, self.small, self.pair.at[1], self.cross)

    def small_away(self):
        self.far.wait()
        self.small[...] += self.pair[1]
        self.second = self.each(3, lambda owner: self.small.at[owner], self.small_in.at[self.here])
        self.small_in[self.here] = self.small[self.here]

    def small_home(self):
        for copy in self.second:
            copy.wait()
        self.small_sum[...] = jnp.sum(self.small_in[...], axis=0)
        self.third = self.each(4, lambda owner: self.small_sum, self.small_out.at[self.here])
        self.small_out[self.here] = self.small_sum[...]

    def big_away(self):
        self.first = self.each(0, lambda owner: self.big.at[owner], self.big_in.at[self.here])
        self.tables = self.each(1, lambda owner: self.table, self.table_in.at[self.here])
        self.big_in[self.here] = self.big[self.here]
        self.table_in[self.here] = self.table[...]

    def finish(self):
        near = self.swap(2, self.gain, self.gain_pair.at[0], self.core)
        near.wait()
        self.gain[...] += self.gain_pair[0]
        far = self.swap(3, self.gain, self.gain_pair.at[1], self.cross)
        far.wait()
        self.gain[...] += self.gain_pair[1]
        gains = self.each(5, lambda owner: self.gain, self.gain_in.at[self.here])
        self.gain_in[self.here] = self.gain[...]
        for copy in self.first:
            copy.wait()
        self.big_sum[...] = jnp.sum(self.big_in[...].astype(jnp.float32), axis=0).astype(jnp.bfloat16)
        last = self.each(2, lambda owner: self.big_sum, self.big_out.at[self.here])
        self.big_out[self.here] = self.big_sum[...]
        for copy in self.tables:
            copy.wait()
        self.table_out[...] = jnp.sum(self.table_in[...], axis=0)
        for copy in gains:
            copy.wait()
        self.gain_out[...] = jnp.sum(self.gain_in[...], axis=0)
        for copy in self.third + last:
            copy.wait()


BIG = (OWNERS, 4 * WIDTH // OWNERS, D)
SMALL = (OWNERS, 8, 256)
TABLE = (8, 128)
SUM_SCRATCH = [
    pltpu.VMEM(BIG, jnp.bfloat16),
    pltpu.VMEM(BIG[1:], jnp.bfloat16),
    pltpu.VMEM((2,) + SMALL, jnp.float32),
    pltpu.VMEM(SMALL, jnp.float32),
    pltpu.VMEM(SMALL[1:], jnp.float32),
    pltpu.VMEM((OWNERS,) + TABLE, jnp.float32),
    pltpu.VMEM((2,) + TABLE, jnp.float32),
    pltpu.VMEM((OWNERS,) + TABLE, jnp.float32),
]
SUM_SEMS = [pltpu.SemaphoreType.DMA((6, 16))] * 2 + [pltpu.SemaphoreType.DMA((4,))] * 2
OUTS = (
    jax.ShapeDtypeStruct(ROW_BLOCK, jnp.bfloat16),
    jax.ShapeDtypeStruct(BIG, jnp.bfloat16),
    jax.ShapeDtypeStruct(SMALL, jnp.float32),
    jax.ShapeDtypeStruct(TABLE, jnp.float32),
    jax.ShapeDtypeStruct(TABLE, jnp.float32),
    jax.ShapeDtypeStruct((2, D, D), jnp.bfloat16),
    jax.ShapeDtypeStruct((2, D, D), jnp.bfloat16),
)
STATE = [
    pltpu.VMEM((MICRO, 4, ROWS, D), jnp.bfloat16),
    pltpu.VMEM((MICRO, 3, LEN, WIDTH), jnp.bfloat16),
    pltpu.VMEM((MICRO, LEN, WIDTH), jnp.bfloat16),
    pltpu.VMEM(ROW_BLOCK, jnp.float32),
    pltpu.VMEM((2, WAVES * WAVE_ROWS, D), jnp.bfloat16),
    pltpu.VMEM((MICRO * ROWS, D), jnp.bfloat16),
    pltpu.VMEM((MICRO * ROWS, EXPERTS), jnp.float32),
    pltpu.VMEM((MICRO * ROWS, 1), jnp.float32),
    pltpu.VMEM((MICRO * ROWS, D), jnp.bfloat16),
    pltpu.VMEM(ROW_BLOCK, jnp.bfloat16),
]
GRADS = [
    pltpu.VMEM(ROW_BLOCK, jnp.bfloat16),
    pltpu.VMEM(ROW_BLOCK, jnp.float32),
    pltpu.VMEM(ROW_BLOCK, jnp.bfloat16),
    pltpu.VMEM((MICRO, 4, ROWS, D), jnp.bfloat16),
    pltpu.VMEM((MICRO, 3, LEN, WIDTH), jnp.bfloat16),
    pltpu.VMEM((8, 2 * LEN), jnp.float32),
    pltpu.VMEM((EXPERTS, D), jnp.float32),
    pltpu.VMEM((1, D), jnp.float32),
    pltpu.VMEM((1, D), jnp.float32),
    pltpu.VMEM(BIG, jnp.bfloat16),
    pltpu.VMEM(SMALL, jnp.float32),
    pltpu.VMEM(TABLE, jnp.float32),
    pltpu.VMEM(TABLE, jnp.float32),
]
WORK = (
    [
        pltpu.VMEM(ROW_BLOCK, jnp.bfloat16),
        pltpu.VMEM((HEADS_HERE, LEN, LEN), jnp.float32),
        pltpu.VMEM((2, D, D), jnp.bfloat16),
        pltpu.VMEM((2, D, D), jnp.bfloat16),
        pltpu.VMEM((4, WAVES, OWNERS, PIECE, HALF), jnp.bfloat16),
        SECTION_SEM,
        SECTION_SEM,
        LOCAL_SEM,
    ]
    + [pltpu.VMEM((2, WAVES * WAVE_ROWS, D), jnp.bfloat16)] * 3
    + [pltpu.VMEM((2, WAVE_ROWS, D), jnp.bfloat16)]
)
INPUTS = 13


def layers_kernel(
    own,
    gains,
    qkv,
    wo,
    rel_table,
    router,
    token_row,
    token_column,
    slot_row,
    slot_column,
    order,
    order_t,
    buckets,
    inner,
    outer,
    *refs,
):
    outs, refs = refs[:7], refs[7:]
    state, refs = refs[:10], refs[10:]
    grads, refs = refs[:13], refs[13:]
    incoming, bias, inner_here, outer_here, arrived, section, section_back, local = refs[:8]
    wide, refs = refs[8:12], refs[12:]
    shard_buffers, slot_buffers, refs = refs[:5], refs[5:13], refs[13:]
    shard_sems, slot_sems, refs = refs[:8], refs[8:20], refs[20:]
    normed_all, packed, mixed, middle, rows, normed_two, router_prob, gating, expert_rows, output = state
    grad_out, middle_grad, input_grad, grad_all, dqkv, offset_grad, router_grad, gain_one, gain_two = grads[:9]
    sources = grads[9:]
    grads_wide, hiddens, pre_grads, results = wide
    gather, heads_sum, part = shard_group(normed_all, shard_buffers, shard_sems)
    gather_back, heads_sum_back, _ = shard_group(grad_all, shard_buffers, shard_sems)
    out, back = slot_exchange(arrived, slot_buffers, slot_sems)
    sums = Sums(sources, outs[1:5], refs[:8], refs[8:])
    keys = (token_row, token_column, slot_row, slot_column)
    first = lax.axis_index("section") == 0
    second = jnp.logical_not(first)
    me = shard_places()[0]

    ready = greet_all()
    fetched = copy_all((inner, outer), (inner_here, outer_here), local, 2)
    offset_grad[...] = lax.dot_general(
        rel_table[...], buckets[...], (NT, ((), ())), precision=lax.Precision.HIGHEST
    )
    fill_bias(offset_grad, bias)
    ready()

    for m in range(MICRO):

        @pl.when(first)
        def _(m=m):
            incoming[m] = own[m]

        @pl.when(second)
        def _(m=m):
            over_section(output, incoming, section, m).wait_recv()

        normed_all[m, me] = rms_norm(incoming[m].astype(jnp.float32), gains[0:1, :]).astype(jnp.bfloat16)
        gather.start(m)
    attend(incoming, qkv, wo, state[:4], bias, gather, heads_sum, part)
    experts(
        middle, gains, router, keys, order, order_t, inner_here, outer_here, fetched, state[4:], arrived, results, out, back
    )
    for stage in (gather, heads_sum, back):
        stage.drain()

    for m in range(MICRO):

        @pl.when(first)
        def _(m=m):
            over_section(output, incoming, section, m).start()

        @pl.when(second)
        def _(m=m):
            outs[0][m] = output[m]
            grad_out[m] = own[m]

    @pl.when(first)
    def _():
        for m in range(MICRO):
            over_section(input_grad, grad_out, section_back, m).wait_recv()

    writes = experts_back(
        grad_out,
        middle,
        normed_two,
        router_prob,
        gating,
        expert_rows,
        gains,
        router,
        keys,
        order,
        order_t,
        inner_here,
        outer_here,
        (outs[5], outs[6], router_grad, gain_two),
        middle_grad,
        arrived,
        (rows, grads_wide, hiddens, pre_grads, results),
        local,
        out,
        back,
    )

    def beside(step):
        if step == 0:
            small = sources[1]
            extra = jnp.concatenate([gain_two[...], jnp.zeros((7, D), jnp.float32)], axis=0)
            for group in range(5):
                block = router_grad[group * 8 : group * 8 + 8, :] if group < 4 else extra
                for third in range(3):
                    small[group * 3 + third] = block[:, third * 256 : (third + 1) * 256]
            small[15] = jnp.zeros(SMALL[1:], jnp.float32)
            sums.small_near()
        if step == 1:
            sums.small_far()
        if step == 2:
            sums.small_away()
        if step == 3:
            sources[2][...] = lax.dot_general(
                offset_grad[...], buckets[...], (((1,), (0,)), ((), ())), precision=lax.Precision.HIGHEST
            )
            sums.small_home()
            sums.big_away()

    def done(m):
        @pl.when(first)
        def _():
            outs[0][m] = input_grad[m]

        @pl.when(second)
        def _():
            over_section(input_grad, grad_out, section_back, m).start()

    attend_back(
        middle_grad,
        incoming,
        gains,
        normed_all,
        packed,
        mixed,
        qkv,
        wo,
        (input_grad, sources[0], offset_grad, gain_one),
        grad_all,
        dqkv,
        bias,
        gather_back,
        heads_sum_back,
        part,
        beside,
        done,
    )
    pieces = [gain_one[:, at : at + 128] for at in range(0, D, 128)]
    sources[3][...] = jnp.concatenate(pieces + [jnp.zeros((2, 128), jnp.float32)], axis=0)
    sums.finish()
    for stage in (back, gather_back, heads_sum_back):
        stage.drain()
    for m in range(MICRO):

        @pl.when(first)
        def _(m=m):
            over_section(output, incoming, section, m).wait_send()

        @pl.when(second)
        def _(m=m):
            over_section(input_grad, grad_out, section_back, m).wait_send()

    for write in writes:
        write.wait()


def both_layers(*arrays):
    return pl.pallas_call(
        layers_kernel,
        out_shape=OUTS,
        in_specs=[VMEM] * INPUTS + [ANY] * 2,
        out_specs=(VMEM,) * 5 + (ANY,) * 2,
        scratch_shapes=STATE
        + GRADS
        + WORK
        + SHARD_BUFFERS
        + SLOT_BUFFERS
        + SHARD_SEMS
        + SLOT_SEMS
        + SUM_SCRATCH
        + SUM_SEMS,
        compiler_params=pltpu.CompilerParams(collective_id=0, has_side_effects=True, vmem_limit_bytes=VMEM_BYTES),
        name="both_layers",
    )(*arrays)


def offset_buckets():
    offsets = np.arange(2 * LEN) - (LEN - 1)
    distance = np.abs(offsets)
    far_bucket = 8 + sum((distance >= threshold).astype(np.int32) for threshold in (12, 16, 23, 32, 46, 64, 91))
    bucket = np.where(distance < 8, distance, far_bucket) + 16 * (offsets > 0)
    return jnp.asarray(bucket[:, None] == np.arange(128)[None, :], jnp.float32)


def slot_keys():
    row = np.arange(WAVES * OWNERS * PIECE)
    half, expert = row % 16 // 8, row % 8 // 4
    slot_row = row // (OWNERS * PIECE) * 4 + row % 4
    return ((half * EXPERTS + row // PIECE % OWNERS * 2 + expert) * (MICRO * CAP) + slot_row).astype(np.int32)


def token_keys(route_ids, slot_ids):
    micro = jnp.arange(MICRO, dtype=jnp.int32)[:, None]
    key = (route_ids * (MICRO * CAP) + micro * CAP + slot_ids).reshape(-1)
    return jnp.concatenate([key, key + EXPERTS * MICRO * CAP])


def per_device(
    stream, norm_gains, attn_qkv, attn_out, rel_bias, router, expert_in, expert_out, routes, slots
):
    rel_table = jnp.pad(rel_bias[0].T, ((0, 5), (0, 96)))
    tokens, slot_rows = token_keys(routes[0], slots[0]), jnp.asarray(slot_keys())
    common = (norm_gains[0], jnp.swapaxes(attn_qkv[0], 1, 2), attn_out[0], rel_table, router[0].T)
    common += (tokens[None, :], tokens[:, None], slot_rows[None, :], slot_rows[:, None])
    common += sorting() + (offset_buckets(), expert_in[0], expert_out[0])
    end_rows, big, small, table, gain_one, inner_grad, outer_grad = both_layers(stream[0], *common)

    big = big.reshape(4, WIDTH, D).astype(jnp.float32)
    small = jnp.swapaxes(small[:15].reshape(5, 3, 8, 256), 1, 2).reshape(40, D)
    return (
        end_rows[None],
        jnp.concatenate([gain_one[:6].reshape(1, D), small[32:33]], axis=0)[None],
        jnp.swapaxes(big[:3], 1, 2)[None],
        big[3][None],
        table[:3, :32].T[None],
        small[:32].T[None],
        inner_grad.astype(jnp.float32)[None],
        outer_grad.astype(jnp.float32)[None],
    )


def solution(mesh):
    return jax.shard_map(
        per_device,
        mesh=mesh,
        in_specs=(
            P("section", None, ("expert", "shard"), None),
            P("section", None, None),
            P("section", None, None, "shard"),
            P("section", "shard", None),
            P("section", None, "shard"),
            P("section", None, None),
            P("section", "expert", None, "shard"),
            P("section", "expert", "shard", None),
            P("section", None, ("expert", "shard")),
            P("section", None, ("expert", "shard")),
        ),
        out_specs=(
            P("section", None, ("expert", "shard"), None),
            P("section", None, None),
            P("section", None, None, "shard"),
            P("section", "shard", None),
            P("section", None, "shard"),
            P("section", None, None),
            P("section", "expert", None, "shard"),
            P("section", "expert", "shard", None),
        ),
        check_vma=False,
    )
```
